32 devices in a mesh: dp: 8 (over y, x, core), tensor: 4 (over z).
Axes of the slice: x: 2, y: 2, z: 4, core: 2. Of those that a mesh axis runs over, the one named last changes fastest.
Arguments:
- layer_input: bfloat16 [8192, 2048], P('dp'), may hold values from -6 to 6
- output_cotangent: bfloat16 [8192, 2048], P('dp'), may hold values from -6 to 6
- block_ids: int32 [8, 1024], P('dp'), may hold values from 0 to 5, never falling along the last dimension, each value on 1 to 256 neighbouring positions
- attention_gain: bfloat16 [2048], P('dp'), may hold values from 0.5 to 1.5
- query_weight: bfloat16 [2048, 2048], P('dp', 'tensor'), may hold values from -0.125 to 0.125
- key_weight: bfloat16 [2048, 2048], P('dp', 'tensor'), may hold values from -0.125 to 0.125
- value_weight: bfloat16 [2048, 2048], P('dp', 'tensor'), may hold values from -0.125 to 0.125
- output_weight: bfloat16 [2048, 2048], P('tensor', 'dp'), may hold values from -0.5 to 0.5
- feedforward_gain: bfloat16 [2048], P('dp'), may hold values from 0.5 to 1.5
- gate_weight: bfloat16 [2048, 8192], P('dp', 'tensor'), may hold values from -0.125 to 0.125
- up_weight: bfloat16 [2048, 8192], P('dp', 'tensor'), may hold values from -0.125 to 0.125
- down_weight: bfloat16 [8192, 2048], P('tensor', 'dp'), may hold values from -0.0625 to 0.0625
Outputs:
- layer_output: bfloat16 [8192, 2048], P('dp')
- input_grad: float32 [8192, 2048], P('dp')
- attention_gain_grad: float32 [2048], P('dp')
- query_weight_grad: float32 [2048, 2048], P('dp', 'tensor')
- key_weight_grad: float32 [2048, 2048], P('dp', 'tensor')
- value_weight_grad: float32 [2048, 2048], P('dp', 'tensor')
- output_weight_grad: float32 [2048, 2048], P('tensor', 'dp')
- feedforward_gain_grad: float32 [2048], P('dp')
- gate_weight_grad: float32 [2048, 8192], P('dp', 'tensor')
- up_weight_grad: float32 [2048, 8192], P('dp', 'tensor')
- down_weight_grad: float32 [8192, 2048], P('tensor', 'dp')
- head_maxima: float32 [32], replicated
- query_clipped: bfloat16 [2048, 2048], P('dp', 'tensor')
- key_clipped: bfloat16 [2048, 2048], P('dp', 'tensor')
The draws below stay inside these ranges and needn't reach their ends.
Inputs may be any that keep to these rules, and one draw needn't show every extreme that they name: `block_ids`: within each sequence the ids never fall; each id covers 1 to 256 consecutive tokens and some id exactly 256.
All inputs are finite; a program needn't handle non-finite values.
Results may differ from the reference program's by a relative error of at most 0.022.
Values may be sent and summed in bfloat16 or wider, within the bound.
No kernel may reach another device: no remote copies, remote signals or barrier semaphores. Data moves between devices by JAX's collectives and lax.ppermute only.
A program may use at most 256 MiB of HBM per device.

```python
import math
import jax
import jax.numpy as jnp
import numpy as np
from jax import lax

D = 2048
HEADS = 32
HEAD_DIM = 64
FF = 8192
SEQ_LEN = 1024
BLOCK = 256
SEQS = 8
TOKENS = 8192


def quiet_columns(key):
    order = jax.random.permutation(key, HEADS)
    scales = jnp.where(order < HEADS // 4, 0.35, 1.0).astype(jnp.float32)
    return jnp.repeat(scales, HEAD_DIM)


def draw_query_weight(key, part):
    columns = quiet_columns(key)
    key = jax.random.fold_in(key, 11)
    entries = jax.random.truncated_normal(key, -4.0, 4.0, (D, D), jnp.float32)
    return (entries * (D // 2) ** (-0.5) * columns[None, :]).astype(jnp.bfloat16)


def draw_key_weight(key, part):
    columns = quiet_columns(key)
    key = jax.random.fold_in(key, 23)
    entries = jax.random.truncated_normal(key, -4.0, 4.0, (D, D), jnp.float32)
    return (entries * (D // 2) ** (-0.5) * columns[None, :]).astype(jnp.bfloat16)


def shard_levels(rng, dims, pieces, low, largest):
    factor_of = 1.0
    for dim, blocks in pieces:
        draws = jax.random.uniform(jax.random.fold_in(jax.random.fold_in(rng, 6), dim), (blocks,), jnp.float32, low / len(pieces), largest / len(pieces))
        factor_of = factor_of * jnp.repeat(jnp.exp(draws), dims[dim] // blocks).reshape((-1,) + (1,) * (len(dims) - 1 - dim))
    return factor_of


def profile(amount, total, reach, slope):
    loads = [(1 << 20) // math.isqrt(grade ** slope) + 1 for grade in range(2, amount + 1)]
    surplus, counts = total - reach - (amount - 1), [1] * (amount - 1)
    while surplus > 0:
        free = [i for i in range(amount - 1) if counts[i] < reach]
        mass, left = sum([loads[i] for i in free]), surplus
        for i in free:
            extra = min(reach - counts[i], max(1, left * loads[i] // mass), surplus)
            counts[i] = counts[i] + extra
            surplus = surplus - extra
    return np.array([reach] + counts)


def uneven_parts(stream_key, number_of, total, most, slope):
    if number_of == 2:
        one = jax.random.randint(stream_key, (), max(1, total - most), min(most, total - 1) + 1)
        return jnp.stack([one, total - one])
    sizes = jnp.asarray(profile(number_of, total, most, slope), jnp.int32)
    couples = (number_of - 1) // 2
    source_of, taker = sizes[1:1 + 2 * couples:2], sizes[2:2 + 2 * couples:2]
    slack = jnp.minimum(source_of - 1, most - taker)
    shifted = jax.random.randint(jax.random.fold_in(stream_key, 1), (couples,), 0, 1 << 20) % (slack + 1)
    sizes = sizes.at[1:1 + 2 * couples:2].set(source_of - shifted).at[2:2 + 2 * couples:2].set(taker + shifted)
    return sizes[jax.random.permutation(jax.random.fold_in(stream_key, 2), number_of)]


def gaussian(rng, shape, scale, limit, pieces=(), kind=jnp.bfloat16):
    values = scale * jax.random.normal(rng, shape, jnp.float32)
    if pieces:
        values = values * shard_levels(rng, shape, pieces, -0.22, 0.18)
    return jnp.clip(values, -limit, limit).astype(kind)


def setup_inputs(seed: int = 0) -> dict:
    streams_of = jax.random.split(jax.random.key(seed), 13)
    layer_input = gaussian(streams_of[0], (TOKENS, D), 1.0, 6.0, ((0, 8),))
    output_cotangent = gaussian(streams_of[1], (TOKENS, D), 1.0, 6.0, ((0, 8),))
    block_ids = jax.vmap(lambda own: jnp.searchsorted(jnp.cumsum(uneven_parts(own, SEQ_LEN // BLOCK + 2, SEQ_LEN, BLOCK, 0)), jnp.arange(SEQ_LEN), side="right"))(jax.random.split(streams_of[2], SEQS)).reshape((SEQS, SEQ_LEN)).astype(jnp.int32)
    attention_gain = jnp.clip(1.0 + 0.1 * jax.random.normal(streams_of[3], (D,), jnp.float32), 0.5, 1.5).astype(jnp.bfloat16)
    query_weight = draw_query_weight(jax.random.fold_in(streams_of[12], 71), 0)
    key_weight = draw_key_weight(jax.random.fold_in(streams_of[12], 71), 0)
    value_weight = gaussian(streams_of[6], (D, D), D ** -0.5, 0.125, ((0, 8), (1, 4)))
    output_weight = gaussian(streams_of[7], (D, D), (D // 16) ** -0.5, 0.5, ((0, 4), (1, 8)))
    feedforward_gain = jnp.clip(1.0 + 0.1 * jax.random.normal(streams_of[8], (D,), jnp.float32), 0.5, 1.5).astype(jnp.bfloat16)
    gate_weight = gaussian(streams_of[9], (D, FF), D ** -0.5, 0.125, ((0, 8), (1, 4)))
    up_weight = gaussian(streams_of[10], (D, FF), D ** -0.5, 0.125, ((0, 8), (1, 4)))
    down_weight = gaussian(streams_of[11], (FF, D), FF ** -0.5, 0.0625, ((0, 4), (1, 8)))
    return {"layer_input": layer_input, "output_cotangent": output_cotangent, "block_ids": block_ids, "attention_gain": attention_gain, "query_weight": query_weight, "key_weight": key_weight, "value_weight": value_weight, "output_weight": output_weight, "feedforward_gain": feedforward_gain, "gate_weight": gate_weight, "up_weight": up_weight, "down_weight": down_weight}


norm_epsilon = 1e-05
rope_theta = 130000.0
clip_tau = 2.0
neg_big = -1e+30

@jax.custom_vjp
def low(v):
    return lax.optimization_barrier(v.astype(jnp.bfloat16)).astype(jnp.float32)

@jax.custom_vjp
def low_back(v):
    return v

def low_keep(v):
    return (low(v), None)

def low_pass(kept, grad):
    return (grad,)

def back_keep(v):
    return (v, None)

def back_low(kept, grad):
    return (low(grad),)
low.defvjp(low_keep, low_pass)
low_back.defvjp(back_keep, back_low)

def rope_tables(length, head_dim):
    half_dim = head_dim // 2
    inverse = rope_theta ** (-(2.0 * jnp.arange(half_dim, dtype=jnp.float32)) / head_dim)
    angles = jnp.arange(length, dtype=jnp.float32)[:, None] * inverse[None, :]
    angles = jnp.concatenate([angles, angles], -1)
    return (jnp.cos(angles)[:, None, :], jnp.sin(angles)[:, None, :])

def rotate_heads(values, cosine, sine):
    half_dim = values.shape[-1] // 2
    turned = jnp.concatenate([-values[..., half_dim:], values[..., :half_dim]], -1)
    return values * cosine + turned * sine

def product(left, right):
    return jnp.dot(left, right, preferred_element_type=jnp.float32, precision=lax.Precision.HIGHEST)

def normalize(values, gain):
    return values * lax.rsqrt(lax.optimization_barrier(jnp.mean(values * values, -1, keepdims=True)) + norm_epsilon) * gain

def layer(inputs, block_row, params, cosine, sine):
    gain_one, query_w, key_w, value_w, output_w, gain_two, gate_w, up_w, down_w = params
    length = inputs.shape[0]
    normed_one = low(normalize(inputs, gain_one))
    queries = low(rotate_heads(low_back(product(normed_one, query_w)).reshape(length, HEADS, HEAD_DIM), cosine, sine))
    keys = low(rotate_heads(low_back(product(normed_one, key_w)).reshape(length, HEADS, HEAD_DIM), cosine, sine))
    values = low_back(low(product(normed_one, value_w))).reshape(length, HEADS, HEAD_DIM)
    visible = block_row[None, :] <= block_row[:, None]

    def attend(parts):
        query_head, key_head, value_head = parts
        scores = low_back(product(query_head, key_head.T) * HEAD_DIM ** (-0.5))
        masked = jnp.where(visible, scores, neg_big)
        peak = lax.optimization_barrier(jnp.max(masked, -1, keepdims=True))
        expo = jnp.exp(masked - peak)
        probs = expo / lax.optimization_barrier(jnp.sum(expo, -1, keepdims=True))
        return (product(low(probs), value_head), jnp.max(peak))
    mixed, peaks = lax.map(jax.checkpoint(attend), (queries.transpose(1, 0, 2), keys.transpose(1, 0, 2), values.transpose(1, 0, 2)))
    attended = low_back(low(mixed.transpose(1, 0, 2).reshape(length, D)))
    resid = inputs + low_back(product(attended, output_w))
    normed_two = low(normalize(resid, gain_two))
    gate = low_back(product(normed_two, gate_w))
    up_proj = low_back(product(normed_two, up_w))
    hidden = low(jax.nn.silu(gate) * up_proj)
    return (resid + low_back(product(hidden, down_w)), peaks)

def reference(layer_input, output_cotangent, block_ids, attention_gain, query_weight, key_weight, value_weight, output_weight, feedforward_gain, gate_weight, up_weight, down_weight):
    params = tuple((weight.astype(jnp.float32) for weight in (attention_gain, query_weight, key_weight, value_weight, output_weight, feedforward_gain, gate_weight, up_weight, down_weight)))
    cosine, sine = rope_tables(SEQ_LEN, HEAD_DIM)
    inputs_all = layer_input.astype(jnp.float32).reshape(SEQS, SEQ_LEN, D)
    cotangent_all = output_cotangent.astype(jnp.float32).reshape(SEQS, SEQ_LEN, D)

    def one_sequence(carry, parts):
        grads, running = carry
        inputs, block_row, cotangent = parts

        def forward(inputs_in, params_in):
            return layer(inputs_in, block_row, params_in, cosine, sine)
        output, pull, peaks = jax.vjp(forward, inputs, params, has_aux=True)
        d_inputs, d_params = pull(cotangent)
        grads = jax.tree.map(jnp.add, grads, d_params)
        return ((grads, jnp.maximum(running, peaks)), (output, d_inputs))
    zeros = jax.tree.map(jnp.zeros_like, params)
    start = jnp.full((HEADS,), neg_big, dtype=jnp.float32)
    (grads, maxima), (outputs, d_inputs) = lax.scan(one_sequence, (zeros, start), (inputs_all, block_ids, cotangent_all))
    factor = jnp.sqrt(clip_tau / jnp.maximum(maxima, clip_tau))
    columns = jnp.repeat(factor, HEAD_DIM)
    query_clipped = (params[1] * columns[None, :]).astype(jnp.bfloat16)
    key_clipped = (params[2] * columns[None, :]).astype(jnp.bfloat16)
    return (outputs.reshape(TOKENS, D).astype(jnp.bfloat16), d_inputs.reshape(TOKENS, D), grads[0], grads[1], grads[2], grads[3], grads[4], grads[5], grads[6], grads[7], grads[8], maxima, query_clipped, key_clipped)
```

```python
import jax
import jax.numpy as jnp
import numpy as np
from jax import lax
from jax.experimental import pallas as pl
from jax.experimental.pallas import tpu as pltpu
from jax.sharding import PartitionSpec as P

HEAD_DIM = 64
BLOCK = 256
LANES = 128
norm_epsilon = 1e-05
rope_theta = 130000.0
clip_tau = 2.0
neg_big = -1e30
f32 = jnp.float32
bf16 = jnp.bfloat16


def mm(a, b):
    return lax.dot_general(a, b, (((1,), (0,)), ((), ())), preferred_element_type=f32)


def mm_nt(a, b):
    return lax.dot_general(a, b, (((1,), (1,)), ((), ())), preferred_element_type=f32)


def mm_tn(a, b):
    return lax.dot_general(a, b, (((0,), (0,)), ((), ())), preferred_element_type=f32)


def rope_tables(length):
    half_dim = HEAD_DIM // 2
    inverse = rope_theta ** (-(2.0 * np.arange(half_dim)) / HEAD_DIM)
    angles = np.tile(np.arange(length)[:, None] * inverse[None, :], (1, LANES // half_dim))
    return jnp.asarray(np.cos(angles), f32), jnp.asarray(np.sin(angles), f32)


def first_half(shape):
    return lax.broadcasted_iota(jnp.int32, shape, 1) % HEAD_DIM < HEAD_DIM // 2


def rotate(values, cosine, sine):
    ahead = pltpu.roll(values, LANES - HEAD_DIM // 2, 1)
    behind = pltpu.roll(values, HEAD_DIM // 2, 1)
    return values * cosine + jnp.where(first_half(values.shape), -ahead, behind) * sine


def unrotate(grads, cosine, sine):
    sined = grads * sine
    ahead = pltpu.roll(sined, LANES - HEAD_DIM // 2, 1)
    behind = pltpu.roll(sined, HEAD_DIM // 2, 1)
    return grads * cosine + jnp.where(first_half(grads.shape), ahead, -behind)


def of_head(values, head):
    lane = lax.broadcasted_iota(jnp.int32, values.shape, 1)
    return jnp.where(lane // HEAD_DIM == head, values, jnp.zeros_like(values))


def hide(scores, ends, start):
    tail = scores[start:]
    key = lax.broadcasted_iota(jnp.int32, tail.shape, 0) + start
    tail = jnp.where(key < ends, tail, neg_big)
    return jnp.concatenate([scores[:start], tail], 0) if start else tail


def fold(combine, values):
    while values.shape[0] % 16 == 0:
        near = values.shape[0] // 2
        values = combine(values[:near], values[near:])
    return values


def forward_kernel(
    q_ref, k_ref, v_ref, cos_ref, sin_ref, end_ref, qo_ref, ko_ref, vo_ref, att_ref, stat_ref
):
    length = q_ref.shape[0]
    cosine, sine = cos_ref[...], sin_ref[...]
    qo_ref[...] = (rotate(q_ref[...], cosine, sine).astype(bf16) * HEAD_DIM ** (-0.5)).astype(bf16)
    ko_ref[...] = rotate(k_ref[...], cosine, sine).astype(bf16)
    values = v_ref[...].astype(bf16)
    vo_ref[...] = values
    lane = lax.broadcasted_iota(jnp.int32, values.shape, 1)
    sides = [jnp.where(lane // HEAD_DIM == head, values, jnp.ones_like(values)) for head in range(2)]
    for start in range(0, length, BLOCK):
        keys = min(length, start + 2 * BLOCK)
        here = slice(start, start + BLOCK)
        tile, ends = qo_ref[here, :], end_ref[:, here]
        mixed = []
        for head in range(2):
            scores = hide(mm_nt(ko_ref[:keys, :], of_head(tile, head)), ends, start)
            peak = jnp.max(fold(jnp.maximum, scores), 0, keepdims=True)
            expo = jnp.exp(scores - peak).astype(bf16)
            product = mm_tn(expo, sides[head][:keys])
            mixed.append(product / pltpu.roll(product, HEAD_DIM, 1))
            row = HEAD_DIM * (1 - head)
            total = jnp.transpose(product)[row : row + 1]
            stat_ref[0, head : head + 1, here] = peak + jnp.log(total)
            stat_ref[0, 2 + head : 3 + head, here] = peak
        att_ref[here, :] = jnp.where(lane[:BLOCK] < HEAD_DIM, mixed[0], mixed[1]).astype(bf16)


def backward_kernel(
    q_ref, k_ref, v_ref, att_ref, da_ref, stat_ref, cos_ref, sin_ref, end_ref, dq_ref, dk_ref, dv_ref, dk_sum, dv_sum
):
    length = q_ref.shape[0]
    turned = jnp.transpose(k_ref[...].astype(f32)).astype(bf16)
    dk_sum[...] = jnp.zeros_like(dk_sum)
    dv_sum[...] = jnp.zeros_like(dv_sum)
    for start in range(0, length, BLOCK):
        keys = min(length, start + 2 * BLOCK)
        here = slice(start, start + BLOCK)
        tile, d_tile = q_ref[here, :], da_ref[here, :]
        ends = end_ref[:, here]
        both = jnp.transpose(att_ref[here, :].astype(f32) * d_tile.astype(f32))
        d_mixed, probs_both, ds_both, tiles, d_tiles = [], [], [], [], []
        for head in range(2):
            tile_head, d_head = of_head(tile, head), of_head(d_tile, head)
            span = slice(head * HEAD_DIM, (head + 1) * HEAD_DIM)
            center = jnp.sum(both[span, :], 0, keepdims=True)
            scores = hide(mm_nt(k_ref[:keys, :], tile_head), ends, start)
            probs = jnp.exp(scores - stat_ref[0, head : head + 1, here])
            d_probs = mm_nt(v_ref[:keys, :], d_head)
            d_scores = (probs * (d_probs - center)).astype(bf16)
            d_mixed.append(mm(turned[span, :keys], d_scores))
            probs_both.append(probs.astype(bf16))
            ds_both.append(d_scores)
            tiles.append(tile_head)
            d_tiles.append(d_head)
        dv_sum[:keys, :] += mm(jnp.concatenate(probs_both, 1), jnp.concatenate(d_tiles, 0))
        dk_sum[:keys, :] += mm(jnp.concatenate(ds_both, 1), jnp.concatenate(tiles, 0))
        d_queries = jnp.transpose(jnp.concatenate(d_mixed, 0)) * HEAD_DIM ** (-0.5)
        dq_ref[here, :] = unrotate(d_queries, cos_ref[here, :], sin_ref[here, :]).astype(bf16)
    dk_ref[...] = unrotate(dk_sum[...], cos_ref[...], sin_ref[...]).astype(bf16)
    dv_ref[...] = dv_sum[...].astype(bf16)


def last_visible(block_row):
    return jnp.sum(block_row[:, None] <= block_row[None, :], 0, dtype=jnp.int32)[None]


def attend_forward(qkv, ends, cosine, sine):
    length, columns = qkv.shape[0], qkv.shape[1] // 3
    pairs = columns // LANES
    spec = lambda base: pl.BlockSpec((length, LANES), lambda p: (0, base + p))
    fixed = lambda shape: pl.BlockSpec(shape, lambda p: (0, 0))
    whole = jax.ShapeDtypeStruct((length, columns), bf16)
    return pl.pallas_call(
        forward_kernel,
        grid=(pairs,),
        in_specs=[spec(0), spec(pairs), spec(2 * pairs)] + [fixed((length, LANES))] * 2 + [fixed((1, length))],
        out_specs=[spec(0)] * 4 + [pl.BlockSpec((1, 8, length), lambda p: (p, 0, 0))],
        out_shape=[whole] * 4 + [jax.ShapeDtypeStruct((pairs, 8, length), f32)],
        compiler_params=pltpu.CompilerParams(vmem_limit_bytes=48 * 2**20),
        cost_estimate=pl.CostEstimate(flops=4 * length * length * columns, bytes_accessed=10 * length * columns * 2, transcendentals=length * length * columns // HEAD_DIM),
        name="attend_forward",
    )(qkv, qkv, qkv, cosine, sine, ends)


def attend_backward(queries, keys, values, attended, d_attended, stats, ends, cosine, sine):
    length, columns = queries.shape
    pairs = columns // LANES
    spec = pl.BlockSpec((length, LANES), lambda p: (0, p))
    fixed = lambda shape: pl.BlockSpec(shape, lambda p: (0, 0))
    whole = jax.ShapeDtypeStruct((length, columns), bf16)
    return pl.pallas_call(
        backward_kernel,
        grid=(pairs,),
        in_specs=[spec] * 5 + [pl.BlockSpec((1, 8, length), lambda p: (p, 0, 0))] + [fixed((length, LANES))] * 2 + [fixed((1, length))],
        out_specs=[spec] * 3,
        out_shape=[whole] * 3,
        scratch_shapes=[pltpu.VMEM((length, LANES), f32)] * 2,
        compiler_params=pltpu.CompilerParams(vmem_limit_bytes=48 * 2**20),
        cost_estimate=pl.CostEstimate(flops=10 * length * length * columns, bytes_accessed=16 * length * columns, transcendentals=length * length * columns // HEAD_DIM),
        name="attend_backward",
    )(queries, keys, values, attended, d_attended, stats, cosine, sine, ends)


def norm_kernel(order_ref, value_ref, hat_ref, same_ref, *, count):
    values = value_ref[...].astype(f32)
    block = value_ref.shape[1] // count
    inverse = lax.rsqrt(jnp.mean(values * values, -1, keepdims=True) + norm_epsilon)
    for place in range(count):
        source = pl.ds(pl.multiple_of(order_ref[place] * block, block), block)
        target = slice(place * block, (place + 1) * block)
        taken = value_ref[:, source]
        same_ref[:, target] = taken
        hat_ref[:, target] = (taken.astype(f32) * inverse).astype(bf16)


def normed_in_order(values, order):
    rows, width = values.shape
    spec = pl.BlockSpec((BLOCK, width), lambda i, order: (i, 0))
    return pl.pallas_call(
        lambda *refs: norm_kernel(*refs, count=order.shape[0]),
        grid_spec=pltpu.PrefetchScalarGridSpec(
            num_scalar_prefetch=1, grid=(rows // BLOCK,), in_specs=[spec], out_specs=[spec] * 2
        ),
        out_shape=[jax.ShapeDtypeStruct(values.shape, bf16)] * 2,
        compiler_params=pltpu.CompilerParams(vmem_limit_bytes=32 * 2**20),
        name="norm_in_order",
    )(order, values)


def move_kernel(order_ref, value_ref, out_ref):
    out_ref[...] = value_ref[...]


def in_order(values, order):
    rows, width = values.shape
    block = (rows, width // order.shape[0])
    return pl.pallas_call(
        move_kernel,
        grid_spec=pltpu.PrefetchScalarGridSpec(
            num_scalar_prefetch=1,
            grid=order.shape,
            in_specs=[pl.BlockSpec(block, lambda p, order: (0, order[p]))],
            out_specs=pl.BlockSpec(block, lambda p, order: (0, p)),
        ),
        out_shape=jax.ShapeDtypeStruct(values.shape, values.dtype),
        name="in_order",
    )(order, values)


def resid_kernel(part_ref, left_ref, right_ref, resid_ref, hat_ref):
    resid = part_ref[...] + mm_nt(left_ref[...], right_ref[...])
    resid_ref[...] = resid
    inverse = lax.rsqrt(jnp.mean(resid * resid, -1, keepdims=True) + norm_epsilon)
    hat_ref[...] = (resid * inverse).astype(bf16)


def resid_and_norm(part, left, right):
    rows, width = part.shape
    spec = pl.BlockSpec((BLOCK, width), lambda i: (i, 0))
    return pl.pallas_call(
        resid_kernel,
        grid=(rows // BLOCK,),
        in_specs=[
            spec,
            pl.BlockSpec((BLOCK, left.shape[1]), lambda i: (i, 0)),
            pl.BlockSpec(right.shape, lambda i: (0, 0)),
        ],
        out_specs=[spec] * 2,
        out_shape=[
            jax.ShapeDtypeStruct(part.shape, f32),
            jax.ShapeDtypeStruct(part.shape, bf16),
        ],
        compiler_params=pltpu.CompilerParams(vmem_limit_bytes=40 * 2**20),
        cost_estimate=pl.CostEstimate(
            flops=2 * rows * width * left.shape[1], bytes_accessed=16 * rows * width, transcendentals=0
        ),
        name="resid_and_norm",
    )(part, left, right)


def after(value, *others):
    return lax.optimization_barrier((value, *others))[0]


def flip(value, mask):
    count = lax.axis_size("dp")
    return lax.ppermute(value, "dp", [(i, i ^ mask) for i in range(count)])


def shift(value, step):
    count = lax.axis_size("tensor")
    return lax.ppermute(value, "tensor", [(i, (i + step) % count) for i in range(count)])


def cross(value, forward):
    masks = (2, 4) if forward else (4, 2)
    return lax.ppermute(value, "dp", [(i, i ^ masks[i % 2]) for i in range(8)])


def gather_order(here, count):
    if count != 8:
        return here ^ jnp.arange(count, dtype=jnp.int32)
    first = jnp.where(here % 2 == 0, 2, 4)
    masks = [0, 1, first, first ^ 1, 6, 7 ^ first, 6 ^ first, 7]
    return here ^ jnp.stack([jnp.asarray(mask, jnp.int32) for mask in masks])


def gather(own):
    count = lax.axis_size("dp")
    if count != 8:
        bit = 1
        while bit < count:
            own = jnp.concatenate([own, flip(own, bit)], 0)
            bit *= 2
        return own, (own,)
    beside = flip(own, 1)
    first = cross(own, True)
    second = cross(beside, True)
    third = cross(first, False)
    most = jnp.concatenate([first, second, third], 0)
    return jnp.concatenate([own, beside, most, flip(most, 1)], 0), (second, third)


def reduced(near, far):
    count = lax.axis_size("dp")
    if count != 8:
        whole = jnp.concatenate([near, far], 0).astype(bf16)
        while count > 1:
            middle = whole.shape[0] // 2
            whole = whole[:middle] + flip(whole[middle:], count // 2)
            count //= 2
        return whole.astype(f32)
    rows = near.shape[0] // 5
    arrived = flip(far.astype(bf16), 1)
    diagonal = (near[4 * rows :] + arrived[2 * rows :].astype(f32)).astype(bf16)
    diagonal = cross(diagonal, False)
    outward = near[2 * rows : 4 * rows] + arrived[: 2 * rows].astype(f32)
    outward = jnp.concatenate(
        [outward[:rows] + diagonal.astype(f32), outward[rows:]], 0
    ).astype(bf16)
    inward = cross(outward, True)
    beside = (near[rows : 2 * rows] + inward[rows:].astype(f32)).astype(bf16)
    return near[:rows] + inward[:rows].astype(f32) + flip(beside, 1).astype(f32)


def ring_gather(own):
    pieces = [own]
    for _ in range(lax.axis_size("tensor") - 1):
        pieces.append(shift(pieces[-1], 1))
    return pieces


def ring_scatter(piece, beside=()):
    count = lax.axis_size("tensor")
    total = piece(1).astype(bf16)
    done = []
    for step in range(2, count + 1):
        arrived = shift(total, 1)
        if step - 2 < len(beside):
            done.append(beside[step - 2](total))
            arrived = after(arrived, done[-1])
        total = arrived.astype(f32) + piece(step % count).astype(f32)
        if step < count:
            total = total.astype(bf16)
    return (total, done) if beside else total


def local(
    layer_input,
    output_cotangent,
    block_ids,
    attention_gain,
    query_weight,
    key_weight,
    value_weight,
    output_weight,
    feedforward_gain,
    gate_weight,
    up_weight,
    down_weight,
):
    tokens, width = layer_input.shape
    here = lax.axis_index("dp")
    place = lax.axis_index("tensor")
    dp_count = lax.axis_size("dp")
    ring = lax.axis_size("tensor")
    part = tokens // ring
    columns = query_weight.shape[1]
    heads_here = columns // HEAD_DIM
    heads = heads_here * ring

    near_order = gather_order(here, dp_count)
    true_order = jnp.argsort(near_order).astype(jnp.int32)

    def token_part(values, owner):
        return lax.dynamic_slice_in_dim(values, owner * part, part, 0)

    gain_one = attention_gain.astype(f32)[:, None]
    gain_two = feedforward_gain.astype(f32)[:, None]
    qkv_weight = jnp.concatenate([query_weight, key_weight, value_weight], 1).astype(f32)
    qkv_all, first = gather((qkv_weight * gain_one).astype(bf16))
    out_own = jnp.transpose(jnp.concatenate(ring_gather(output_weight), 0))
    out_all, first = gather(after(out_own, *first))
    gate_all, first = gather(after((gate_weight.astype(f32) * gain_two).astype(bf16), *first))
    up_all, first = gather(after((up_weight.astype(f32) * gain_two).astype(bf16), *first))
    down_all, first = gather(after(jnp.transpose(down_weight), *first))

    hat, inputs = normed_in_order(layer_input, near_order)
    cot = in_order(output_cotangent, near_order)
    cosine, sine = rope_tables(tokens)
    ends = last_visible(block_ids[0])
    queries, keys, values, attended, stats = attend_forward(mm(hat, qkv_all), ends, cosine, sine)
    pieces = ring_gather(attended)

    local_peak = jnp.max(stats[:, 2:4], -1).reshape(heads_here)
    bit = 1
    while bit < dp_count:
        local_peak = jnp.maximum(local_peak, flip(local_peak, bit))
        bit *= 2
    peak_pieces = jnp.concatenate(
        [local_peak] + [shift(local_peak, step) for step in range(1, ring)]
    )
    order = (place - jnp.arange(heads) // heads_here) % ring * heads_here
    head_maxima = peak_pieces[order + jnp.arange(heads) % heads_here]
    factor = jnp.sqrt(clip_tau / jnp.maximum(local_peak, clip_tau))
    factors = jnp.repeat(factor, HEAD_DIM)[None, :]
    query_clipped = (query_weight.astype(f32) * factors).astype(bf16)
    key_clipped = (key_weight.astype(f32) * factors).astype(bf16)

    most = jnp.concatenate(pieces[:-1], 1)
    resid_most = inputs.astype(f32) + mm_nt(most, out_all[:, : most.shape[1]])
    resid, hat_two = resid_and_norm(resid_most, pieces[-1], out_all[:, most.shape[1] :])
    gate = mm(hat_two, gate_all)
    up = mm(hat_two, up_all)
    sigma = jax.nn.sigmoid(gate)
    swish = gate * sigma
    hidden = (swish * up).astype(bf16)
    d_hidden = mm(cot, down_all)
    d_gate = (d_hidden * up * sigma * (1.0 + gate * (1.0 - sigma))).astype(bf16)
    d_up = (d_hidden * swish).astype(bf16)

    def mid_grad(t):
        owner = (place - t) % ring
        return mm_nt(token_part(d_gate, owner), gate_all) + mm_nt(token_part(d_up, owner), up_all)

    near_width = width // 8 * 5 if dp_count == 8 else width // 2

    def grad_blocks(left, right):
        return mm_tn(left[:, :near_width], right), mm_tn(left[:, near_width:], right).astype(bf16)

    def down_work(ready):
        return grad_blocks(cot, after(hidden, ready))

    def gate_work(ready):
        return grad_blocks(after(hat_two, ready), d_gate)

    def up_work(ready):
        return grad_blocks(after(hat_two, ready), d_up)

    scaled_two, halves = ring_scatter(mid_grad, (down_work, gate_work, up_work))
    down_grad = jnp.transpose(reduced(*halves[0]))
    gate_sum = reduced(*halves[1])
    up_sum = reduced(*halves[2])
    resid_part, cot_part = token_part(resid, place), token_part(cot, place)
    inv_part = lax.rsqrt(jnp.mean(resid_part * resid_part, -1, keepdims=True) + norm_epsilon)
    d_resid = (
        cot_part.astype(f32)
        + inv_part * scaled_two
        - resid_part * inv_part**3 * jnp.mean(scaled_two * resid_part, -1, keepdims=True)
    )
    d_attn = d_resid.astype(bf16)
    d_att = mm(d_attn, out_all).astype(bf16)
    d_pieces = [d_att[:, :columns]] + [
        shift(d_att[:, t * columns : (t + 1) * columns], -t) for t in range(1, ring)
    ]
    d_attended = jnp.zeros((tokens, columns), bf16)
    for t, piece in enumerate(d_pieces):
        d_attended = lax.dynamic_update_slice(d_attended, piece, ((place + t) % ring * part, 0))

    def out_piece(t):
        return mm_nt(token_part(hidden, (place - t) % ring), down_all)

    def spread(values, dtype):
        whole = jnp.zeros((tokens, width), dtype)
        for t, piece in enumerate(ring_gather(values)):
            start = (place - t) % ring * part
            whole = lax.dynamic_update_slice(whole, piece.astype(dtype), (start, 0))
        return whole

    out_part = (resid_part + ring_scatter(out_piece)).astype(bf16)
    layer_output = spread(in_order(out_part, true_order), bf16)

    d_query, d_key, d_value = attend_backward(
        queries, keys, values, attended, d_attended, stats, ends, cosine, sine
    )
    d_qkv = jnp.concatenate([d_query, d_key, d_value], 1)

    def in_grad(t):
        return mm_nt(token_part(d_qkv, (place - t) % ring), qkv_all)

    att_part = jnp.concatenate([token_part(piece, place) for piece in pieces], 1)

    def out_work(ready):
        return grad_blocks(after(d_attn, ready), att_part)

    def qkv_work(ready):
        return grad_blocks(after(hat, ready), d_qkv)

    scaled_one, halves = ring_scatter(in_grad, (qkv_work, out_work))
    qkv_sum = reduced(*halves[0])
    out_sum = jnp.transpose(reduced(*halves[1]))
    output_grad = ring_scatter(lambda t: out_sum[t * columns : (t + 1) * columns])
    input_part = token_part(inputs, place).astype(f32)
    inv_part = lax.rsqrt(jnp.mean(input_part * input_part, -1, keepdims=True) + norm_epsilon)
    input_back = (
        d_resid
        + inv_part * scaled_one
        - input_part * inv_part**3 * jnp.mean(scaled_one * input_part, -1, keepdims=True)
    )
    input_grad = spread(in_order(input_back.astype(bf16), true_order), f32)
    qkv_grad = qkv_sum * gain_one

    gains = jnp.stack(
        [
            jnp.sum(qkv_sum * qkv_weight, 1),
            jnp.sum(gate_sum * gate_weight.astype(f32), 1)
            + jnp.sum(up_sum * up_weight.astype(f32), 1),
        ]
    )
    gain_pieces = jnp.stack([gains] + [shift(gains, step) for step in range(1, ring)])
    gain_sum = jnp.sum(jnp.take(gain_pieces, (place - jnp.arange(ring)) % ring, axis=0), 0)

    return (
        layer_output,
        input_grad,
        gain_sum[0],
        qkv_grad[:, :columns],
        qkv_grad[:, columns : 2 * columns],
        qkv_grad[:, 2 * columns :],
        output_grad,
        gain_sum[1],
        gate_sum * gain_two,
        up_sum * gain_two,
        down_grad,
        head_maxima,
        query_clipped,
        key_clipped,
    )


def solution(mesh):
    in_specs = (
        P("dp", None),
        P("dp", None),
        P("dp", None),
        P("dp"),
        P("dp", "tensor"),
        P("dp", "tensor"),
        P("dp", "tensor"),
        P("tensor", "dp"),
        P("dp"),
        P("dp", "tensor"),
        P("dp", "tensor"),
        P("tensor", "dp"),
    )
    out_specs = (
        P("dp", None),
        P("dp", None),
        P("dp"),
        P("dp", "tensor"),
        P("dp", "tensor"),
        P("dp", "tensor"),
        P("tensor", "dp"),
        P("dp"),
        P("dp", "tensor"),
        P("dp", "tensor"),
        P("tensor", "dp"),
        P(),
        P("dp", "tensor"),
        P("dp", "tensor"),
    )
    return jax.shard_map(local, mesh=mesh, in_specs=in_specs, out_specs=out_specs, check_vma=False)
```

```python
import jax
import jax.numpy as jnp
import numpy as np
from jax import lax
from jax.experimental import pallas as pl
from jax.experimental.pallas import tpu as pltpu
from jax.sharding import PartitionSpec as P

HEAD_DIM = 64
BLOCK = 256
LANES = 128
norm_epsilon = 1e-05
rope_theta = 130000.0
clip_tau = 2.0
neg_big = -1e30
f32 = jnp.float32
bf16 = jnp.bfloat16


def mm(a, b):
    return lax.dot_general(a, b, (((1,), (0,)), ((), ())), preferred_element_type=f32)


def mm_nt(a, b):
    return lax.dot_general(a, b, (((1,), (1,)), ((), ())), preferred_element_type=f32)


def mm_tn(a, b):
    return lax.dot_general(a, b, (((0,), (0,)), ((), ())), preferred_element_type=f32)


def rope_tables(length):
    half_dim = HEAD_DIM // 2
    inverse = rope_theta ** (-(2.0 * np.arange(half_dim)) / HEAD_DIM)
    angles = np.tile(np.arange(length)[:, None] * inverse[None, :], (1, LANES // half_dim))
    return jnp.asarray(np.cos(angles), f32), jnp.asarray(np.sin(angles), f32)


def first_half(shape):
    return lax.broadcasted_iota(jnp.int32, shape, 1) % HEAD_DIM < HEAD_DIM // 2


def rotate(values, cosine, sine):
    ahead = pltpu.roll(values, LANES - HEAD_DIM // 2, 1)
    behind = pltpu.roll(values, HEAD_DIM // 2, 1)
    return values * cosine + jnp.where(first_half(values.shape), -ahead, behind) * sine


def unrotate(grads, cosine, sine):
    sined = grads * sine
    ahead = pltpu.roll(sined, LANES - HEAD_DIM // 2, 1)
    behind = pltpu.roll(sined, HEAD_DIM // 2, 1)
    return grads * cosine + jnp.where(first_half(grads.shape), ahead, -behind)


def of_head(values, head):
    lane = lax.broadcasted_iota(jnp.int32, values.shape, 1)
    return jnp.where(lane // HEAD_DIM == head, values, jnp.zeros_like(values))


def hide(scores, ends, start):
    tail = scores[start:]
    key = lax.broadcasted_iota(jnp.int32, tail.shape, 0) + start
    tail = jnp.where(key < ends, tail, neg_big)
    return jnp.concatenate([scores[:start], tail], 0) if start else tail


def fold(combine, values):
    while values.shape[0] % 16 == 0:
        near = values.shape[0] // 2
        values = combine(values[:near], values[near:])
    return values


def forward_kernel(
    q_ref, k_ref, v_ref, cos_ref, sin_ref, end_ref, qo_ref, ko_ref, vo_ref, att_ref, stat_ref
):
    length = q_ref.shape[0]
    cosine, sine = cos_ref[...], sin_ref[...]
    qo_ref[...] = (rotate(q_ref[...], cosine, sine).astype(bf16) * HEAD_DIM ** (-0.5)).astype(bf16)
    ko_ref[...] = rotate(k_ref[...], cosine, sine).astype(bf16)
    values = v_ref[...].astype(bf16)
    vo_ref[...] = values
    lane = lax.broadcasted_iota(jnp.int32, values.shape, 1)
    sides = [jnp.where(lane // HEAD_DIM == head, values, jnp.ones_like(values)) for head in range(2)]
    for start in range(0, length, BLOCK):
        keys = min(length, start + 2 * BLOCK)
        here = slice(start, start + BLOCK)
        tile, ends = qo_ref[here, :], end_ref[:, here]
        mixed = []
        for head in range(2):
            scores = hide(mm_nt(ko_ref[:keys, :], of_head(tile, head)), ends, start)
            peak = jnp.max(fold(jnp.maximum, scores), 0, keepdims=True)
            expo = jnp.exp(scores - peak).astype(bf16)
            product = mm_tn(expo, sides[head][:keys])
            mixed.append(product / pltpu.roll(product, HEAD_DIM, 1))
            row = HEAD_DIM * (1 - head)
            total = jnp.transpose(product)[row : row + 1]
            stat_ref[0, head : head + 1, here] = peak + jnp.log(total)
            stat_ref[0, 2 + head : 3 + head, here] = peak
        att_ref[here, :] = jnp.where(lane[:BLOCK] < HEAD_DIM, mixed[0], mixed[1]).astype(bf16)


def backward_kernel(
    q_ref, k_ref, v_ref, att_ref, da_ref, stat_ref, cos_ref, sin_ref, end_ref, dq_ref, dk_ref, dv_ref, dk_sum, dv_sum
):
    length = q_ref.shape[0]
    turned = jnp.transpose(k_ref[...].astype(f32)).astype(bf16)
    dk_sum[...] = jnp.zeros_like(dk_sum)
    dv_sum[...] = jnp.zeros_like(dv_sum)
    for start in range(0, length, BLOCK):
        keys = min(length, start + 2 * BLOCK)
        here = slice(start, start + BLOCK)
        tile, d_tile = q_ref[here, :], da_ref[here, :]
        ends = end_ref[:, here]
        both = jnp.transpose(att_ref[here, :].astype(f32) * d_tile.astype(f32))
        d_mixed, probs_both, ds_both, tiles, d_tiles = [], [], [], [], []
        for head in range(2):
            tile_head, d_head = of_head(tile, head), of_head(d_tile, head)
            span = slice(head * HEAD_DIM, (head + 1) * HEAD_DIM)
            center = jnp.sum(both[span, :], 0, keepdims=True)
            scores = hide(mm_nt(k_ref[:keys, :], tile_head), ends, start)
            probs = jnp.exp(scores - stat_ref[0, head : head + 1, here])
            d_probs = mm_nt(v_ref[:keys, :], d_head)
            d_scores = (probs * (d_probs - center)).astype(bf16)
            d_mixed.append(mm(turned[span, :keys], d_scores))
            probs_both.append(probs.astype(bf16))
            ds_both.append(d_scores)
            tiles.append(tile_head)
            d_tiles.append(d_head)
        dv_sum[:keys, :] += mm(jnp.concatenate(probs_both, 1), jnp.concatenate(d_tiles, 0))
        dk_sum[:keys, :] += mm(jnp.concatenate(ds_both, 1), jnp.concatenate(tiles, 0))
        d_queries = jnp.transpose(jnp.concatenate(d_mixed, 0)) * HEAD_DIM ** (-0.5)
        dq_ref[here, :] = unrotate(d_queries, cos_ref[here, :], sin_ref[here, :]).astype(bf16)
    dk_ref[...] = unrotate(dk_sum[...], cos_ref[...], sin_ref[...]).astype(bf16)
    dv_ref[...] = dv_sum[...].astype(bf16)


def last_visible(block_row):
    return jnp.sum(block_row[:, None] <= block_row[None, :], 0, dtype=jnp.int32)[None]


def attend_forward(qkv, ends, cosine, sine):
    length, columns = qkv.shape[0], qkv.shape[1] // 3
    pairs = columns // LANES
    spec = lambda base: pl.BlockSpec((length, LANES), lambda p: (0, base + p))
    fixed = lambda shape: pl.BlockSpec(shape, lambda p: (0, 0))
    whole = jax.ShapeDtypeStruct((length, columns), bf16)
    return pl.pallas_call(
        forward_kernel,
        grid=(pairs,),
        in_specs=[spec(0), spec(pairs), spec(2 * pairs)] + [fixed((length, LANES))] * 2 + [fixed((1, length))],
        out_specs=[spec(0)] * 4 + [pl.BlockSpec((1, 8, length), lambda p: (p, 0, 0))],
        out_shape=[whole] * 4 + [jax.ShapeDtypeStruct((pairs, 8, length), f32)],
        compiler_params=pltpu.CompilerParams(vmem_limit_bytes=48 * 2**20),
        cost_estimate=pl.CostEstimate(flops=4 * length * length * columns, bytes_accessed=10 * length * columns * 2, transcendentals=length * length * columns // HEAD_DIM),
        name="attend_forward",
    )(qkv, qkv, qkv, cosine, sine, ends)


def attend_backward(queries, keys, values, attended, d_attended, stats, ends, cosine, sine):
    length, columns = queries.shape
    pairs = columns // LANES
    spec = pl.BlockSpec((length, LANES), lambda p: (0, p))
    fixed = lambda shape: pl.BlockSpec(shape, lambda p: (0, 0))
    whole = jax.ShapeDtypeStruct((length, columns), bf16)
    return pl.pallas_call(
        backward_kernel,
        grid=(pairs,),
        in_specs=[spec] * 5 + [pl.BlockSpec((1, 8, length), lambda p: (p, 0, 0))] + [fixed((length, LANES))] * 2 + [fixed((1, length))],
        out_specs=[spec] * 3,
        out_shape=[whole] * 3,
        scratch_shapes=[pltpu.VMEM((length, LANES), f32)] * 2,
        compiler_params=pltpu.CompilerParams(vmem_limit_bytes=48 * 2**20),
        cost_estimate=BESIDE,
        name="attend_backward",
    )(queries, keys, values, attended, d_attended, stats, cosine, sine, ends)


def norm_kernel(order_ref, value_ref, hat_ref, same_ref, true_ref, *, count):
    values = value_ref[...].astype(f32)
    block = value_ref.shape[1] // count
    inverse = lax.rsqrt(jnp.mean(values * values, -1, keepdims=True) + norm_epsilon)
    true_ref[...] = (values * inverse).astype(bf16)
    for place in range(count):
        source = pl.ds(pl.multiple_of(order_ref[place] * block, block), block)
        target = slice(place * block, (place + 1) * block)
        same_ref[:, target] = value_ref[:, source]
        hat_ref[:, target] = true_ref[:, source]


def normed_in_order(values, order):
    rows, width = values.shape
    spec = pl.BlockSpec((BLOCK, width), lambda i, order: (i, 0))
    return pl.pallas_call(
        lambda *refs: norm_kernel(*refs, count=order.shape[0]),
        grid_spec=pltpu.PrefetchScalarGridSpec(
            num_scalar_prefetch=1, grid=(rows // BLOCK,), in_specs=[spec], out_specs=[spec] * 3
        ),
        out_shape=[jax.ShapeDtypeStruct(values.shape, bf16)] * 3,
        compiler_params=pltpu.CompilerParams(vmem_limit_bytes=32 * 2**20),
        name="norm_in_order",
    )(order, values)


def move_kernel(order_ref, value_ref, out_ref, *, count):
    block = value_ref.shape[1] // count
    for place in range(count):
        source = pl.ds(pl.multiple_of(order_ref[place] * block, block), block)
        out_ref[:, place * block : (place + 1) * block] = value_ref[:, source]


def in_order(values, order):
    rows, width = values.shape
    spec = pl.BlockSpec((min(rows, BLOCK), width), lambda i, order: (i, 0))
    return pl.pallas_call(
        lambda *refs: move_kernel(*refs, count=order.shape[0]),
        grid_spec=pltpu.PrefetchScalarGridSpec(
            num_scalar_prefetch=1, grid=(rows // min(rows, BLOCK),), in_specs=[spec], out_specs=spec
        ),
        out_shape=jax.ShapeDtypeStruct(values.shape, values.dtype),
        name="in_order",
    )(order, values)


def resid_kernel(place_ref, order_ref, part_ref, left_ref, right_ref, resid_ref, hat_ref, true_ref, *, count):
    resid = part_ref[...] + mm_nt(left_ref[...], right_ref[...])
    block = resid.shape[1] // count
    inverse = lax.rsqrt(jnp.mean(resid * resid, -1, keepdims=True) + norm_epsilon)
    hat_ref[...] = (resid * inverse).astype(bf16)
    for place in range(count):
        source = pl.ds(pl.multiple_of(order_ref[place] * block, block), block)
        true_ref[:, place * block : (place + 1) * block] = hat_ref[:, source]

    @pl.when(pl.program_id(0) == place_ref[0])
    def _():
        resid_ref[...] = resid


def resid_and_norm(part, left, right, place, order, rows):
    tokens, width = part.shape
    spec = pl.BlockSpec((rows, width), lambda i, place, order: (i, 0))
    return pl.pallas_call(
        lambda *refs: resid_kernel(*refs, count=order.shape[0]),
        grid_spec=pltpu.PrefetchScalarGridSpec(
            num_scalar_prefetch=2,
            grid=(tokens // rows,),
            in_specs=[
                spec,
                pl.BlockSpec((rows, left.shape[1]), lambda i, place, order: (i, 0)),
                pl.BlockSpec(right.shape, lambda i, place, order: (0, 0)),
            ],
            out_specs=[pl.BlockSpec((rows, width), lambda i, place, order: (0, 0)), spec, spec],
        ),
        out_shape=[
            jax.ShapeDtypeStruct((rows, width), f32),
            jax.ShapeDtypeStruct(part.shape, bf16),
            jax.ShapeDtypeStruct(part.shape, bf16),
        ],
        compiler_params=pltpu.CompilerParams(vmem_limit_bytes=40 * 2**20),
        cost_estimate=pl.CostEstimate(
            flops=2 * tokens * width * left.shape[1], bytes_accessed=10 * tokens * width, transcendentals=0
        ),
        name="resid_and_norm",
    )(place.reshape(1), order, part, left, right)


def stack_kernel(*refs, groups):
    *refs, held, arrived, left = refs
    pieces, wholes = refs[:-groups], refs[-groups:]
    inward, outward = [], []
    start = 0
    for index, piece in enumerate(pieces):
        rows = piece.shape[0] // groups
        inward.append(
            pltpu.make_async_copy(piece, held.at[pl.ds(groups * start, groups * rows)], arrived.at[index])
        )
        outward.append(
            [
                pltpu.make_async_copy(
                    held.at[pl.ds(groups * start + group * rows, rows)],
                    whole.at[pl.ds(start, rows)],
                    left.at[index, group],
                )
                for group, whole in enumerate(wholes)
            ]
        )
        start += rows
    for copy in inward:
        copy.start()
    for one, several in zip(inward, outward):
        one.wait()
        for copy in several:
            copy.start()
    for several in outward:
        for copy in several:
            copy.wait()


def stack(pieces, groups):
    rows, width = sum(piece.shape[0] for piece in pieces), pieces[0].shape[1]
    dtype = pieces[0].dtype
    anywhere = pl.BlockSpec(memory_space=pl.ANY)
    return pl.pallas_call(
        lambda *refs: stack_kernel(*refs, groups=groups),
        in_specs=[anywhere] * len(pieces),
        out_specs=[anywhere] * groups,
        out_shape=[jax.ShapeDtypeStruct((rows // groups, width), dtype)] * groups,
        scratch_shapes=[
            pltpu.VMEM((rows, width), dtype),
            pltpu.SemaphoreType.DMA((len(pieces),)),
            pltpu.SemaphoreType.DMA((len(pieces), groups)),
        ],
        compiler_params=pltpu.CompilerParams(vmem_limit_bytes=32 * 2**20),
        cost_estimate=pl.CostEstimate(flops=0, bytes_accessed=rows * width // 8, transcendentals=0),
        name="stack",
    )(*pieces)


BESIDE = pl.CostEstimate(flops=4 * 2**30, bytes_accessed=2**20, transcendentals=0)


def grad_kernel(left_ref, right_ref, *refs, far):
    near_ref, far_ref = refs[-2:]
    product = mm_tn(left_ref[...], right_ref[...]).astype(bf16)

    @pl.when(pl.program_id(0) < far)
    def _():
        far_ref[...] = product

    @pl.when(pl.program_id(0) >= far)
    def _():
        near_ref[...] = product


def grad_beside(left, right, share, which, groups, into):
    (depth, rows), columns = left.shape, right.shape[1]
    near, far = share[0], share[1] - share[0]
    tile = rows // share[1]
    anywhere = pl.BlockSpec(memory_space=pl.ANY)
    return pl.pallas_call(
        lambda *refs: grad_kernel(*refs, far=far),
        grid=(near + far,),
        in_specs=[
            pl.BlockSpec((depth, tile), lambda i: (0, jnp.where(i < far, near + i, i - far))),
            pl.BlockSpec(right.shape, lambda i: (0, 0)),
        ]
        + [anywhere] * len(into),
        out_specs=[
            pl.BlockSpec((tile, columns), lambda i: (jnp.maximum(i - far, 0) * groups + which, 0)),
            pl.BlockSpec((tile, columns), lambda i: (jnp.minimum(i, far - 1) * groups + which, 0)),
        ],
        out_shape=[
            jax.ShapeDtypeStruct((near * groups * tile, columns), bf16),
            jax.ShapeDtypeStruct((far * groups * tile, columns), bf16),
        ],
        input_output_aliases={2 + k: k for k in range(len(into))},
        compiler_params=pltpu.CompilerParams(vmem_limit_bytes=56 * 2**20),
        cost_estimate=BESIDE,
        name="grad_beside",
    )(left, right, *into)


def tn_kernel(left_ref, right_ref, out_ref):
    out_ref[...] = mm_tn(left_ref[...], right_ref[...]).astype(bf16)


def plain_beside(left, right):
    (depth, rows), columns = left.shape, right.shape[1]
    tile = 2 * BLOCK
    return pl.pallas_call(
        tn_kernel,
        grid=(rows // tile,),
        in_specs=[
            pl.BlockSpec((depth, tile), lambda i: (0, i)),
            pl.BlockSpec(right.shape, lambda i: (0, 0)),
        ],
        out_specs=pl.BlockSpec((tile, columns), lambda i: (i, 0)),
        out_shape=jax.ShapeDtypeStruct((rows, columns), bf16),
        compiler_params=pltpu.CompilerParams(vmem_limit_bytes=56 * 2**20),
        cost_estimate=BESIDE,
        name="plain_beside",
    )(left, right)


def nt_kernel(left_ref, right_ref, out_ref):
    out_ref[...] = mm_nt(left_ref[...], right_ref[...]).astype(bf16)


def product_beside(left, right):
    (rows, depth), columns = left.shape, right.shape[0]
    tile = 2 * BLOCK
    return pl.pallas_call(
        nt_kernel,
        grid=(columns // tile,),
        in_specs=[
            pl.BlockSpec(left.shape, lambda i: (0, 0)),
            pl.BlockSpec((tile, depth), lambda i: (i, 0)),
        ],
        out_specs=pl.BlockSpec((rows, tile), lambda i: (0, i)),
        out_shape=jax.ShapeDtypeStruct((rows, columns), bf16),
        compiler_params=pltpu.CompilerParams(vmem_limit_bytes=56 * 2**20),
        cost_estimate=BESIDE,
        name="product_beside",
    )(left, right)


def mid_kernel(hat_ref, up_ref, gate_ref, dh_ref, hidden_ref, dg_ref, du_ref):
    up = mm(hat_ref[...], up_ref[...])
    gate, d_hidden = gate_ref[...], dh_ref[...]
    sigma = 1.0 / (1.0 + jnp.exp(-gate))
    swish = gate * sigma
    hidden_ref[...] = (swish * up).astype(bf16)
    dg_ref[...] = (d_hidden * up * (sigma + swish * (1.0 - sigma))).astype(bf16)
    du_ref[...] = (d_hidden * swish).astype(bf16)


def mid_layer(hat, up_weight, gate, d_hidden):
    (rows, depth), columns = hat.shape, up_weight.shape[1]
    tile = min(2 * BLOCK, columns)
    spec = pl.BlockSpec((rows, tile), lambda i: (0, i))
    return pl.pallas_call(
        mid_kernel,
        grid=(columns // tile,),
        in_specs=[
            pl.BlockSpec(hat.shape, lambda i: (0, 0)),
            pl.BlockSpec((depth, tile), lambda i: (0, i)),
            spec,
            spec,
        ],
        out_specs=[spec] * 3,
        out_shape=[jax.ShapeDtypeStruct((rows, columns), bf16)] * 3,
        compiler_params=pltpu.CompilerParams(vmem_limit_bytes=56 * 2**20),
        cost_estimate=pl.CostEstimate(
            flops=2 * rows * depth * columns, bytes_accessed=20 * rows * columns, transcendentals=rows * columns
        ),
        name="mid_layer",
    )(hat, up_weight, gate, d_hidden)


def pair_kernel(a_ref, b_ref, c_ref, d_ref, out_ref):
    out_ref[...] = (mm_nt(a_ref[...], b_ref[...]) + mm_nt(c_ref[...], d_ref[...])).astype(bf16)


def pair_product(a, b, c, d):
    (rows, depth), columns = a.shape, b.shape[0]
    tile = 2 * BLOCK
    whole = pl.BlockSpec(a.shape, lambda i: (0, 0))
    part = pl.BlockSpec((tile, depth), lambda i: (i, 0))
    return pl.pallas_call(
        pair_kernel,
        grid=(columns // tile,),
        in_specs=[whole, part, whole, part],
        out_specs=pl.BlockSpec((rows, tile), lambda i: (0, i)),
        out_shape=jax.ShapeDtypeStruct((rows, columns), bf16),
        compiler_params=pltpu.CompilerParams(vmem_limit_bytes=56 * 2**20),
        cost_estimate=pl.CostEstimate(
            flops=4 * rows * depth * columns, bytes_accessed=12 * rows * columns, transcendentals=0
        ),
        name="pair_product",
    )(a, b, c, d)


def after(value, *others):
    return lax.optimization_barrier((value, *others))[0]


def flip(value, mask):
    count = lax.axis_size("dp")
    return lax.ppermute(value, "dp", [(i, i ^ mask) for i in range(count)])


def shift(value, step):
    count = lax.axis_size("tensor")
    return lax.ppermute(value, "tensor", [(i, (i + step) % count) for i in range(count)])


def cross(value, forward):
    masks = (2, 4) if forward else (4, 2)
    return lax.ppermute(value, "dp", [(i, i ^ masks[i % 2]) for i in range(8)])


def gather_order(here, count):
    if count != 8:
        return here ^ jnp.arange(count, dtype=jnp.int32)
    first = jnp.where(here % 2 == 0, 2, 4)
    masks = [0, 1, first, first ^ 1, 6, 7 ^ first, 6 ^ first, 7]
    return here ^ jnp.stack([jnp.asarray(mask, jnp.int32) for mask in masks])


class Order:
    def __init__(self):
        self.last = ()

    def run(self, work, *inputs):
        inputs, _ = lax.optimization_barrier((inputs, self.last))
        result = work(*inputs)
        self.last = jax.tree.leaves(result)
        return result

    def wait(self, *moving):
        moving, _ = lax.optimization_barrier((moving, self.last))
        self.last = jax.tree.leaves(moving)
        return moving if len(moving) > 1 else moving[0]


def double(own):
    bit = 1
    while bit < lax.axis_size("dp"):
        own = jnp.concatenate([own, flip(own, bit)], 0)
        bit *= 2
    return own


class Gather:
    def __init__(self, order, own):
        self.order, self.own, self.count = order, own, lax.axis_size("dp")

    def pair(self):
        if self.count == 8:
            self.beside = flip(self.own, 1)

    def begin(self, own_too=True):
        if self.count == 8:
            if own_too:
                self.own, self.beside = self.order.wait(self.own, self.beside)
                self.first = cross(self.own, True)
            else:
                self.beside = self.order.wait(self.beside)
            self.second = cross(self.beside, True)

    def early(self):
        if self.count == 8:
            self.first = cross(self.own, True)

    def middle(self, with_second=False):
        if self.count == 8:
            if with_second:
                self.first, self.second = self.order.wait(self.first, self.second)
            else:
                self.first = self.order.wait(self.first)
            self.third = cross(self.first, False)

    def late(self):
        if self.count == 8:
            self.second, self.third = self.order.wait(self.second, self.third)
            self.flipped = [flip(piece, 1) for piece in (self.first, self.second, self.third)]

    def end(self, groups=1):
        if self.count == 8:
            flipped = self.order.wait(*self.flipped)
            pieces = (self.own, self.beside, self.first, self.second, self.third, *flipped)
            whole = self.order.run(lambda *pieces: stack(pieces, groups), *pieces)
            return whole if groups > 1 else whole[0]
        return double(self.own)


class Ring:
    def __init__(self, order, terms, owner_part):
        self.order, self.count = order, lax.axis_size("tensor")
        self.terms, self.part, self.stage = terms, owner_part, 1
        sent = order.run(lambda terms: self.part(terms, 1), terms)
        self.moving = shift(sent, 1)

    def step(self):
        if self.stage == self.count:
            return
        self.stage += 1
        arrived = self.arrived = self.order.wait(self.moving)

        def add(arrived, terms):
            total = arrived.astype(f32) + self.part(terms, self.stage % self.count).astype(f32)
            return total.astype(bf16) if self.stage < self.count else total

        total = self.order.run(add, arrived, self.terms)
        if self.stage < self.count:
            self.moving = shift(total, 1)
        else:
            self.result = total

    def finish(self):
        while self.stage < self.count:
            self.step()
        return self.result


class Line:
    def __init__(self, order, terms, owner_part):
        self.order, self.terms, self.part = order, terms, owner_part
        self.count, self.place, self.stage = lax.axis_size("tensor"), lax.axis_index("tensor"), 0
        self.step()

    def send(self, value, up):
        pairs = [(i, i + 1) for i in range(self.count - 1) if i < self.stage]
        if not up:
            pairs = [(self.count - 1 - i, self.count - 1 - j) for i, j in pairs]
        return lax.ppermute(value, "tensor", pairs)

    def step(self):
        if self.stage == self.count:
            return
        arrived = self.order.wait(*self.moving) if self.stage else ()
        self.stage += 1
        if self.stage == self.count:
            self.result = self.order.run(
                lambda terms, up, down: self.part(terms, 0).astype(f32)
                + up.astype(f32)
                + down.astype(f32),
                self.terms,
                *arrived,
            )
            return
        ahead = self.count - self.stage
        owners = jnp.minimum(self.place + ahead, self.count - 1), jnp.maximum(self.place - ahead, 0)

        def add(terms, *arrived):
            values = [self.part(terms, (self.place - owner) % self.count) for owner in owners]
            if arrived:
                values = [a.astype(f32) + b.astype(f32) for a, b in zip(values, arrived)]
            return [value.astype(bf16) for value in values]

        up, down = self.order.run(add, self.terms, *arrived)
        self.moving = self.send(up, True), self.send(down, False)

    def finish(self):
        while self.stage < self.count:
            self.step()
        return self.result


class Spread:
    def __init__(self, order, own):
        self.order, self.own = order, own
        self.count, self.place, self.stage = lax.axis_size("tensor"), lax.axis_index("tensor"), 0
        self.arrived = [(own, own)]
        self.go()

    def go(self):
        up, down = self.arrived[-1]
        pairs = [(i, i + 1) for i in range(self.count - 1) if i >= self.stage]
        back = [(self.count - 1 - i, self.count - 1 - j) for i, j in pairs]
        self.moving = lax.ppermute(up, "tensor", pairs), lax.ppermute(down, "tensor", back)
        self.stage += 1

    def step(self):
        if len(self.arrived) < self.count:
            self.arrived.append(self.order.wait(*self.moving))
            if self.stage < self.count - 1:
                self.go()

    def whole(self, dtype):
        rows, width = self.own.shape
        result = jnp.zeros((rows * self.count, width), dtype)
        for t in range(self.count):
            value = self.own
            if t:
                up, down = self.arrived[t][0], self.arrived[self.count - t][1]
                value = jnp.where(self.place >= t, up, down)
            start = (self.place - t) % self.count * rows
            result = lax.dynamic_update_slice(result, value.astype(dtype), (start, 0))
        return result


def local(
    layer_input,
    output_cotangent,
    block_ids,
    attention_gain,
    query_weight,
    key_weight,
    value_weight,
    output_weight,
    feedforward_gain,
    gate_weight,
    up_weight,
    down_weight,
):
    tokens, width = layer_input.shape
    here = lax.axis_index("dp")
    place = lax.axis_index("tensor")
    dp_count = lax.axis_size("dp")
    ring = lax.axis_size("tensor")
    part = tokens // ring
    columns = query_weight.shape[1]
    heads_here = columns // HEAD_DIM
    heads = heads_here * ring

    near_order = gather_order(here, dp_count)
    true_order = jnp.argsort(near_order).astype(jnp.int32)

    def token_part(values, owner):
        return lax.dynamic_slice_in_dim(values, owner * part, part, 0)

    gain_one = attention_gain.astype(f32)[:, None]
    gain_two = feedforward_gain.astype(f32)[:, None]
    qkv_weight = jnp.concatenate([query_weight, key_weight, value_weight], 1).astype(f32)
    order = Order()
    run, wait = order.run, order.wait

    def ring_part(values, t):
        return token_part(values, (place - t) % ring)

    qkv_gather = Gather(order, run(lambda w, g: (w * g).astype(bf16), qkv_weight, gain_one))
    qkv_gather.early()
    qkv_gather.pair()
    out_moving = [shift(output_weight, step) for step in range(1, ring)]
    gate_own = run(lambda w, g: (w.astype(f32) * g).astype(bf16), gate_weight, gain_two)
    up_own = run(lambda w, g: (w.astype(f32) * g).astype(bf16), up_weight, gain_two)
    qkv_gather.begin(False)
    hat, inputs, hat_true = run(normed_in_order, layer_input, near_order)
    qkv_gather.middle(True)
    out_pieces = wait(*out_moving)
    both_own = run(
        lambda down, *pieces: (jnp.transpose(jnp.concatenate(pieces, 0)), jnp.transpose(down)),
        down_weight,
        output_weight,
        *out_pieces,
    )
    paired = dp_count == 8 and both_own[0].shape == both_own[1].shape
    both_gather = Gather(order, jnp.concatenate(both_own, 0) if paired else both_own[0])
    both_gather.pair()
    gate_gather, up_gather = Gather(order, gate_own), Gather(order, up_own)
    qkv_gather.late()
    both_gather.begin()
    qkv_all = qkv_gather.end()

    qkv = run(mm, hat, qkv_all)
    cosine, sine = rope_tables(tokens)
    ends = last_visible(block_ids[0])
    queries, keys, values, attended, stats = run(attend_forward, qkv, ends, cosine, sine)
    moving = shift(attended, 1)
    pieces = [attended]
    gate_gather.pair()
    up_gather.pair()
    cot = run(in_order, output_cotangent, near_order)
    both_gather.middle()
    while len(pieces) < ring - 1:
        pieces.append(wait(moving))
        moving = shift(pieces[-1], 1)
        if len(pieces) == 2:
            gate_gather.begin()
            gate_gather.middle()
    both_gather.late()
    up_gather.begin()
    if paired:
        out_all, down_all = both_gather.end(2)
    else:
        out_all, down_all = both_gather.end(), double(both_own[1])
    most = jnp.concatenate(pieces, 1)
    resid_most = run(
        lambda inputs, most, weight: inputs.astype(f32) + mm_nt(most, weight[:, : most.shape[1]]),
        inputs,
        most,
        out_all,
    )
    pieces.append(wait(moving))
    gate_gather.late()

    resid_part, hat_two, hat_two_true = run(
        lambda most, last, weight, place: resid_and_norm(
            most, last, weight[:, weight.shape[1] - columns :], place, true_order, part
        ),
        resid_most,
        pieces[-1],
        out_all,
        place,
    )
    up_gather.middle()
    d_hidden = run(mm, cot, down_all)
    gate_all = gate_gather.end()
    gate = run(mm, hat_two, gate_all)
    up_gather.late()
    up_all = up_gather.end()

    hidden, d_gate, d_up = run(mid_layer, hat_two, up_all, gate, d_hidden)
    d_mid = run(pair_product, d_gate, gate_all, d_up, up_all)

    def scaled(total, weight, gain):
        total = total.astype(f32)
        return total * gain, jnp.sum(total * weight.astype(f32), 1)

    def to_sum(grad, *before):
        grad = after(grad, *before) if before else grad
        return lax.psum_scatter(grad, "dp", scatter_dimension=0, tiled=True)

    back = Ring(order, d_mid, ring_part)
    local_peak = jnp.max(stats[:, 2:4], -1).reshape(heads_here)
    peaks = [local_peak, 1]

    def peak_step():
        if peaks[1] < dp_count:
            peaks[0] = jnp.maximum(peaks[0], wait(flip(peaks[0], peaks[1])))
            peaks[1] *= 2

    gate_grad = run(plain_beside, hat_two_true, d_gate)
    peak_step()
    back.step()
    gate_moving = to_sum(gate_grad, back.arrived)
    up_grad = run(plain_beside, hat_two_true, d_up)
    peak_step()
    back.step()
    up_moving = to_sum(up_grad, gate_grad, back.arrived)
    mlp = run(product_beside, hidden, down_all)
    down_grad = run(plain_beside, output_cotangent, hidden)
    peak_step()
    scaled_two = back.finish()
    down_moving = to_sum(down_grad, up_grad, back.arrived)
    while peaks[1] < dp_count:
        peak_step()
    local_peak = peaks[0]
    forth = Ring(order, mlp, ring_part)

    def first_norm_back(scaled, resid, cot):
        inverse = lax.rsqrt(jnp.mean(resid * resid, -1, keepdims=True) + norm_epsilon)
        back = resid * inverse**3 * jnp.mean(scaled * resid, -1, keepdims=True)
        return token_part(cot, place).astype(f32) + inverse * scaled - back

    d_resid = run(first_norm_back, scaled_two, resid_part, cot)
    d_attn = d_resid.astype(bf16)
    d_att = run(lambda a, b: mm(a, b).astype(bf16), d_attn, out_all)
    d_moving = [shift(d_att[:, t * columns : (t + 1) * columns], -t) for t in range(1, ring)]
    def unite(*pieces):
        whole = jnp.zeros((tokens, columns), bf16)
        for t, piece in enumerate(pieces):
            whole = lax.dynamic_update_slice(whole, piece, ((place + t) % ring * part, 0))
        return whole

    d_pieces = wait(*d_moving)
    d_attended = run(unite, d_att[:, :columns], *d_pieces)

    def in_true_order(*pieces):
        parts = [token_part(piece, place) for piece in pieces[::-1]]
        both = jnp.concatenate(parts + parts, 0)
        whole = lax.dynamic_slice_in_dim(both, (ring - 1 - place) * part, tokens, 0)
        return jnp.concatenate(jnp.split(whole, ring, 0), 1)

    forth.step()

    def in_true_order(*pieces):
        parts = [token_part(piece, place) for piece in pieces[::-1]]
        both = jnp.concatenate(parts + parts, 0)
        whole = lax.dynamic_slice_in_dim(both, (ring - 1 - place) * part, tokens, 0)
        return jnp.concatenate(jnp.split(whole, ring, 0), 1)

    parts = run(
        attend_backward, queries, keys, values, attended, d_attended, stats, ends, cosine, sine
    )
    forth.step()
    d_qkv, d_in = run(
        lambda weight, *parts: (
            jnp.concatenate(parts, 1),
            mm_nt(jnp.concatenate(parts, 1), weight).astype(bf16),
        ),
        qkv_all,
        *parts,
    )
    qkv_grad = run(plain_beside, hat_true, d_qkv)
    out_part = run(
        lambda a, b, c: in_order((a + b).astype(bf16), c), resid_part, forth.finish(), true_order
    )
    qkv_moving = to_sum(qkv_grad, down_grad, forth.arrived)
    layer_out = Spread(order, out_part)
    att_part = run(in_true_order, *pieces)
    d_attn_true = run(in_order, d_attn, true_order)
    out_grad = run(plain_beside, d_attn_true, att_part)
    layer_out.step()
    back = Line(order, d_in, ring_part)
    out_moving = to_sum(out_grad, qkv_grad, *layer_out.arrived[1])
    back.step()
    layer_out.step()
    back.step()
    while len(layer_out.arrived) < ring:
        layer_out.step()
    scaled_one = back.finish()

    def second_norm_back(scaled, inputs, d_resid, true_order):
        values = token_part(inputs, place).astype(f32)
        inverse = lax.rsqrt(jnp.mean(values * values, -1, keepdims=True) + norm_epsilon)
        back = values * inverse**3 * jnp.mean(scaled * values, -1, keepdims=True)
        return in_order((d_resid + inverse * scaled - back).astype(bf16), true_order)

    in_part = run(second_norm_back, scaled_one, inputs, d_resid, true_order)
    moving, in_pieces = shift(in_part, 1), [in_part]
    layer_output = run(lambda: layer_out.whole(bf16))
    input_grad = jnp.zeros((tokens, width), f32)

    def place_piece(whole, piece):
        start = (place - len(in_pieces) + 1) % ring * part
        return lax.dynamic_update_slice(whole, piece.astype(f32), (start, 0))

    input_grad = run(place_piece, input_grad, in_part)
    while len(in_pieces) < ring:
        in_pieces.append(wait(moving))
        if len(in_pieces) < ring:
            moving = shift(in_pieces[-1], 1)
            input_grad = run(place_piece, input_grad, in_pieces[-1])
            if len(in_pieces) == 2:
                gate_result = run(scaled, wait(gate_moving), gate_weight, gain_two)
                up_result = run(scaled, wait(up_moving), up_weight, gain_two)
                down_result = run(lambda a: jnp.transpose(a.astype(f32)), wait(down_moving))
            else:
                qkv_result = run(scaled, wait(qkv_moving), qkv_weight, gain_one)
                out_rows = run(jnp.transpose, wait(out_moving))

    small = jnp.concatenate(
        [
            qkv_result[1],
            gate_result[1] + up_result[1],
            local_peak,
            jnp.zeros((LANES - heads_here,), f32),
        ]
    )
    small_moving = [shift(small, step) for step in range(1, ring)]

    def heads_of(owner):
        return lax.dynamic_slice_in_dim(out_rows, owner * columns, columns, 0)

    out_moving = [shift(heads_of((place + step) % ring), step) for step in range(1, ring)]
    input_grad = run(place_piece, input_grad, in_pieces[-1])
    smalls = [small, *wait(*small_moving)]
    share = width // dp_count
    peak_pieces = [piece[2 * share : 2 * share + heads_here] for piece in smalls]
    gain_sum = jnp.take(jnp.stack(smalls), (place - jnp.arange(ring)) % ring, axis=0)
    gain_sum = jnp.sum(gain_sum[:, : 2 * share].reshape(ring, 2, share), 0)
    output_grad = heads_of(place).astype(f32)
    for moved in wait(*out_moving):
        output_grad = output_grad + moved.astype(f32)
    qkv_grad = qkv_result[0]

    spots = (place - jnp.arange(heads) // heads_here) % ring * heads_here
    head_maxima = jnp.concatenate(peak_pieces)[spots + jnp.arange(heads) % heads_here]
    factor = jnp.sqrt(clip_tau / jnp.maximum(local_peak, clip_tau))
    factors = jnp.repeat(factor, HEAD_DIM)[None, :]
    query_clipped = (query_weight.astype(f32) * factors).astype(bf16)
    key_clipped = (key_weight.astype(f32) * factors).astype(bf16)

    return (
        layer_output,
        input_grad,
        gain_sum[0],
        qkv_grad[:, :columns],
        qkv_grad[:, columns : 2 * columns],
        qkv_grad[:, 2 * columns :],
        output_grad,
        gain_sum[1],
        gate_result[0],
        up_result[0],
        down_result,
        head_maxima,
        query_clipped,
        key_clipped,
    )


def solution(mesh):
    in_specs = (
        P("dp", None),
        P("dp", None),
        P("dp", None),
        P("dp"),
        P("dp", "tensor"),
        P("dp", "tensor"),
        P("dp", "tensor"),
        P("tensor", "dp"),
        P("dp"),
        P("dp", "tensor"),
        P("dp", "tensor"),
        P("tensor", "dp"),
    )
    out_specs = (
        P("dp", None),
        P("dp", None),
        P("dp"),
        P("dp", "tensor"),
        P("dp", "tensor"),
        P("dp", "tensor"),
        P("tensor", "dp"),
        P("dp"),
        P("dp", "tensor"),
        P("dp", "tensor"),
        P("tensor", "dp"),
        P(),
        P("dp", "tensor"),
        P("dp", "tensor"),
    )
    return jax.shard_map(local, mesh=mesh, in_specs=in_specs, out_specs=out_specs, check_vma=False)
```

```python
import jax
import jax.numpy as jnp
import numpy as np
from jax import lax
from jax.experimental import pallas as pl
from jax.experimental.pallas import tpu as pltpu
from jax.sharding import PartitionSpec as P

HEAD_DIM = 64
BLOCK = 256
LANES = 128
norm_epsilon = 1e-05
rope_theta = 130000.0
clip_tau = 2.0
neg_big = -1e30
f32 = jnp.float32
bf16 = jnp.bfloat16


def mm(a, b):
    return lax.dot_general(a, b, (((1,), (0,)), ((), ())), preferred_element_type=f32)


def mm_nt(a, b):
    return lax.dot_general(a, b, (((1,), (1,)), ((), ())), preferred_element_type=f32)


def mm_tn(a, b):
    return lax.dot_general(a, b, (((0,), (0,)), ((), ())), preferred_element_type=f32)


def rope_tables(length):
    half_dim = HEAD_DIM // 2
    inverse = rope_theta ** (-(2.0 * np.arange(half_dim)) / HEAD_DIM)
    angles = np.tile(np.arange(length)[:, None] * inverse[None, :], (1, LANES // half_dim))
    return jnp.asarray(np.cos(angles), f32), jnp.asarray(np.sin(angles), f32)


def first_half(shape):
    return lax.broadcasted_iota(jnp.int32, shape, 1) % HEAD_DIM < HEAD_DIM // 2


def rotate(values, cosine, sine):
    ahead = pltpu.roll(values, LANES - HEAD_DIM // 2, 1)
    behind = pltpu.roll(values, HEAD_DIM // 2, 1)
    return values * cosine + jnp.where(first_half(values.shape), -ahead, behind) * sine


def unrotate(grads, cosine, sine):
    sined = grads * sine
    ahead = pltpu.roll(sined, LANES - HEAD_DIM // 2, 1)
    behind = pltpu.roll(sined, HEAD_DIM // 2, 1)
    return grads * cosine + jnp.where(first_half(grads.shape), ahead, -behind)


def of_head(values, head):
    lane = lax.broadcasted_iota(jnp.int32, values.shape, 1)
    return jnp.where(lane // HEAD_DIM == head, values, jnp.zeros_like(values))


def hide(scores, ends, start):
    tail = scores[start:]
    key = lax.broadcasted_iota(jnp.int32, tail.shape, 0) + start
    tail = jnp.where(key < ends, tail, neg_big)
    return jnp.concatenate([scores[:start], tail], 0) if start else tail


def fold(combine, values):
    while values.shape[0] % 16 == 0:
        near = values.shape[0] // 2
        values = combine(values[:near], values[near:])
    return values


def forward_kernel(
    q_ref, k_ref, v_ref, cos_ref, sin_ref, end_ref, qo_ref, ko_ref, vo_ref, att_ref, stat_ref
):
    length = q_ref.shape[0]
    cosine, sine = cos_ref[...], sin_ref[...]
    qo_ref[...] = (rotate(q_ref[...], cosine, sine).astype(bf16) * HEAD_DIM ** (-0.5)).astype(bf16)
    ko_ref[...] = rotate(k_ref[...], cosine, sine).astype(bf16)
    values = v_ref[...].astype(bf16)
    vo_ref[...] = values
    lane = lax.broadcasted_iota(jnp.int32, values.shape, 1)
    sides = [jnp.where(lane // HEAD_DIM == head, values, jnp.ones_like(values)) for head in range(2)]
    for start in range(0, length, BLOCK):
        keys = min(length, start + 2 * BLOCK)
        here = slice(start, start + BLOCK)
        tile, ends = qo_ref[here, :], end_ref[:, here]
        mixed = []
        for head in range(2):
            scores = hide(mm_nt(ko_ref[:keys, :], of_head(tile, head)), ends, start)
            peak = jnp.max(fold(jnp.maximum, scores), 0, keepdims=True)
            expo = jnp.exp(scores - peak).astype(bf16)
            product = mm_tn(expo, sides[head][:keys])
            mixed.append(product / pltpu.roll(product, HEAD_DIM, 1))
            row = HEAD_DIM * (1 - head)
            total = jnp.transpose(product)[row : row + 1]
            stat_ref[0, head : head + 1, here] = peak + jnp.log(total)
            stat_ref[0, 2 + head : 3 + head, here] = peak
        att_ref[here, :] = jnp.where(lane[:BLOCK] < HEAD_DIM, mixed[0], mixed[1]).astype(bf16)


def backward_kernel(
    q_ref, k_ref, v_ref, att_ref, da_ref, stat_ref, cos_ref, sin_ref, end_ref, dq_ref, dk_ref, dv_ref, dk_sum, dv_sum
):
    length = q_ref.shape[0]
    turned = jnp.transpose(k_ref[...].astype(f32)).astype(bf16)
    dk_sum[...] = jnp.zeros_like(dk_sum)
    dv_sum[...] = jnp.zeros_like(dv_sum)
    for start in range(0, length, BLOCK):
        keys = min(length, start + 2 * BLOCK)
        here = slice(start, start + BLOCK)
        tile, d_tile = q_ref[here, :], da_ref[here, :]
        ends = end_ref[:, here]
        both = jnp.transpose(att_ref[here, :].astype(f32) * d_tile.astype(f32))
        d_mixed, probs_both, ds_both, tiles, d_tiles = [], [], [], [], []
        for head in range(2):
            tile_head, d_head = of_head(tile, head), of_head(d_tile, head)
            span = slice(head * HEAD_DIM, (head + 1) * HEAD_DIM)
            center = jnp.sum(both[span, :], 0, keepdims=True)
            scores = hide(mm_nt(k_ref[:keys, :], tile_head), ends, start)
            probs = jnp.exp(scores - stat_ref[0, head : head + 1, here])
            d_probs = mm_nt(v_ref[:keys, :], d_head)
            d_scores = (probs * (d_probs - center)).astype(bf16)
            d_mixed.append(mm(turned[span, :keys], d_scores))
            probs_both.append(probs.astype(bf16))
            ds_both.append(d_scores)
            tiles.append(tile_head)
            d_tiles.append(d_head)
        dv_sum[:keys, :] += mm(jnp.concatenate(probs_both, 1), jnp.concatenate(d_tiles, 0))
        dk_sum[:keys, :] += mm(jnp.concatenate(ds_both, 1), jnp.concatenate(tiles, 0))
        d_queries = jnp.transpose(jnp.concatenate(d_mixed, 0)) * HEAD_DIM ** (-0.5)
        dq_ref[here, :] = unrotate(d_queries, cos_ref[here, :], sin_ref[here, :]).astype(bf16)
    dk_ref[...] = unrotate(dk_sum[...], cos_ref[...], sin_ref[...]).astype(bf16)
    dv_ref[...] = dv_sum[...].astype(bf16)


def last_visible(block_row):
    return jnp.sum(block_row[:, None] <= block_row[None, :], 0, dtype=jnp.int32)[None]


def attend_forward(qkv, ends, cosine, sine):
    length, columns = qkv.shape[0], qkv.shape[1] // 3
    pairs = columns // LANES
    spec = lambda base: pl.BlockSpec((length, LANES), lambda p: (0, base + p))
    fixed = lambda shape: pl.BlockSpec(shape, lambda p: (0, 0))
    whole = jax.ShapeDtypeStruct((length, columns), bf16)
    return pl.pallas_call(
        forward_kernel,
        grid=(pairs,),
        in_specs=[spec(0), spec(pairs), spec(2 * pairs)] + [fixed((length, LANES))] * 2 + [fixed((1, length))],
        out_specs=[spec(0)] * 4 + [pl.BlockSpec((1, 8, length), lambda p: (p, 0, 0))],
        out_shape=[whole] * 4 + [jax.ShapeDtypeStruct((pairs, 8, length), f32)],
        compiler_params=pltpu.CompilerParams(vmem_limit_bytes=48 * 2**20),
        cost_estimate=pl.CostEstimate(flops=4 * length * length * columns, bytes_accessed=10 * length * columns * 2, transcendentals=length * length * columns // HEAD_DIM),
        name="attend_forward",
    )(qkv, qkv, qkv, cosine, sine, ends)


def attend_backward(queries, keys, values, attended, d_attended, stats, ends, cosine, sine):
    length, columns = queries.shape
    pairs = columns // LANES
    spec = pl.BlockSpec((length, LANES), lambda p: (0, p))
    fixed = lambda shape: pl.BlockSpec(shape, lambda p: (0, 0))
    whole = jax.ShapeDtypeStruct((length, columns), bf16)
    return pl.pallas_call(
        backward_kernel,
        grid=(pairs,),
        in_specs=[spec] * 5 + [pl.BlockSpec((1, 8, length), lambda p: (p, 0, 0))] + [fixed((length, LANES))] * 2 + [fixed((1, length))],
        out_specs=[spec] * 3,
        out_shape=[whole] * 3,
        scratch_shapes=[pltpu.VMEM((length, LANES), f32)] * 2,
        compiler_params=pltpu.CompilerParams(vmem_limit_bytes=48 * 2**20),
        cost_estimate=BESIDE,
        name="attend_backward",
    )(queries, keys, values, attended, d_attended, stats, cosine, sine, ends)


def norm_kernel(order_ref, value_ref, hat_ref, same_ref, true_ref, *, count):
    values = value_ref[...].astype(f32)
    block = value_ref.shape[1] // count
    inverse = lax.rsqrt(jnp.mean(values * values, -1, keepdims=True) + norm_epsilon)
    true_ref[...] = (values * inverse).astype(bf16)
    for place in range(count):
        source = pl.ds(pl.multiple_of(order_ref[place] * block, block), block)
        target = slice(place * block, (place + 1) * block)
        same_ref[:, target] = value_ref[:, source]
        hat_ref[:, target] = true_ref[:, source]


def normed_in_order(values, order):
    rows, width = values.shape
    spec = pl.BlockSpec((BLOCK, width), lambda i, order: (i, 0))
    return pl.pallas_call(
        lambda *refs: norm_kernel(*refs, count=order.shape[0]),
        grid_spec=pltpu.PrefetchScalarGridSpec(
            num_scalar_prefetch=1, grid=(rows // BLOCK,), in_specs=[spec], out_specs=[spec] * 3
        ),
        out_shape=[jax.ShapeDtypeStruct(values.shape, bf16)] * 3,
        compiler_params=pltpu.CompilerParams(vmem_limit_bytes=32 * 2**20),
        name="norm_in_order",
    )(order, values)


def move_kernel(order_ref, value_ref, out_ref, *, count):
    block = value_ref.shape[1] // count
    for place in range(count):
        source = pl.ds(pl.multiple_of(order_ref[place] * block, block), block)
        out_ref[:, place * block : (place + 1) * block] = value_ref[:, source]


def in_order(values, order):
    rows, width = values.shape
    spec = pl.BlockSpec((min(rows, BLOCK), width), lambda i, order: (i, 0))
    return pl.pallas_call(
        lambda *refs: move_kernel(*refs, count=order.shape[0]),
        grid_spec=pltpu.PrefetchScalarGridSpec(
            num_scalar_prefetch=1, grid=(rows // min(rows, BLOCK),), in_specs=[spec], out_specs=spec
        ),
        out_shape=jax.ShapeDtypeStruct(values.shape, values.dtype),
        name="in_order",
    )(order, values)


def resid_kernel(place_ref, order_ref, part_ref, left_ref, right_ref, resid_ref, hat_ref, true_ref, *, count):
    resid = part_ref[...] + mm_nt(left_ref[...], right_ref[...])
    block = resid.shape[1] // count
    inverse = lax.rsqrt(jnp.mean(resid * resid, -1, keepdims=True) + norm_epsilon)
    hat_ref[...] = (resid * inverse).astype(bf16)
    for place in range(count):
        source = pl.ds(pl.multiple_of(order_ref[place] * block, block), block)
        true_ref[:, place * block : (place + 1) * block] = hat_ref[:, source]

    @pl.when(pl.program_id(0) == place_ref[0])
    def _():
        resid_ref[...] = resid


def resid_and_norm(part, left, right, place, order, rows):
    tokens, width = part.shape
    spec = pl.BlockSpec((rows, width), lambda i, place, order: (i, 0))
    return pl.pallas_call(
        lambda *refs: resid_kernel(*refs, count=order.shape[0]),
        grid_spec=pltpu.PrefetchScalarGridSpec(
            num_scalar_prefetch=2,
            grid=(tokens // rows,),
            in_specs=[
                spec,
                pl.BlockSpec((rows, left.shape[1]), lambda i, place, order: (i, 0)),
                pl.BlockSpec(right.shape, lambda i, place, order: (0, 0)),
            ],
            out_specs=[pl.BlockSpec((rows, width), lambda i, place, order: (0, 0)), spec, spec],
        ),
        out_shape=[
            jax.ShapeDtypeStruct((rows, width), f32),
            jax.ShapeDtypeStruct(part.shape, bf16),
            jax.ShapeDtypeStruct(part.shape, bf16),
        ],
        compiler_params=pltpu.CompilerParams(vmem_limit_bytes=40 * 2**20),
        cost_estimate=pl.CostEstimate(
            flops=2 * tokens * width * left.shape[1], bytes_accessed=10 * tokens * width, transcendentals=0
        ),
        name="resid_and_norm",
    )(place.reshape(1), order, part, left, right)


def stack_kernel(*refs, groups):
    *refs, held, arrived, left = refs
    pieces, wholes = refs[:-groups], refs[-groups:]
    inward, outward = [], []
    start = 0
    for index, piece in enumerate(pieces):
        rows = piece.shape[0] // groups
        inward.append(
            pltpu.make_async_copy(piece, held.at[pl.ds(groups * start, groups * rows)], arrived.at[index])
        )
        outward.append(
            [
                pltpu.make_async_copy(
                    held.at[pl.ds(groups * start + group * rows, rows)],
                    whole.at[pl.ds(start, rows)],
                    left.at[index, group],
                )
                for group, whole in enumerate(wholes)
            ]
        )
        start += rows
    for copy in inward:
        copy.start()
    for one, several in zip(inward, outward):
        one.wait()
        for copy in several:
            copy.start()
    for several in outward:
        for copy in several:
            copy.wait()


def stack(pieces, groups):
    rows, width = sum(piece.shape[0] for piece in pieces), pieces[0].shape[1]
    dtype = pieces[0].dtype
    anywhere = pl.BlockSpec(memory_space=pl.ANY)
    return pl.pallas_call(
        lambda *refs: stack_kernel(*refs, groups=groups),
        in_specs=[anywhere] * len(pieces),
        out_specs=[anywhere] * groups,
        out_shape=[jax.ShapeDtypeStruct((rows // groups, width), dtype)] * groups,
        scratch_shapes=[
            pltpu.VMEM((rows, width), dtype),
            pltpu.SemaphoreType.DMA((len(pieces),)),
            pltpu.SemaphoreType.DMA((len(pieces), groups)),
        ],
        compiler_params=pltpu.CompilerParams(vmem_limit_bytes=32 * 2**20),
        cost_estimate=pl.CostEstimate(flops=0, bytes_accessed=rows * width // 8, transcendentals=0),
        name="stack",
    )(*pieces)


BESIDE = pl.CostEstimate(flops=4 * 2**30, bytes_accessed=2**20, transcendentals=0)


def grad_kernel(left_ref, right_ref, *refs, far):
    near_ref, far_ref = refs[-2:]
    product = mm_tn(left_ref[...], right_ref[...]).astype(bf16)

    @pl.when(pl.program_id(0) < far)
    def _():
        far_ref[...] = product

    @pl.when(pl.program_id(0) >= far)
    def _():
        near_ref[...] = product


def grad_beside(left, right, share, which, groups, into):
    (depth, rows), columns = left.shape, right.shape[1]
    near, far = share[0], share[1] - share[0]
    tile = rows // share[1]
    anywhere = pl.BlockSpec(memory_space=pl.ANY)
    return pl.pallas_call(
        lambda *refs: grad_kernel(*refs, far=far),
        grid=(near + far,),
        in_specs=[
            pl.BlockSpec((depth, tile), lambda i: (0, jnp.where(i < far, near + i, i - far))),
            pl.BlockSpec(right.shape, lambda i: (0, 0)),
        ]
        + [anywhere] * len(into),
        out_specs=[
            pl.BlockSpec((tile, columns), lambda i: (jnp.maximum(i - far, 0) * groups + which, 0)),
            pl.BlockSpec((tile, columns), lambda i: (jnp.minimum(i, far - 1) * groups + which, 0)),
        ],
        out_shape=[
            jax.ShapeDtypeStruct((near * groups * tile, columns), bf16),
            jax.ShapeDtypeStruct((far * groups * tile, columns), bf16),
        ],
        input_output_aliases={2 + k: k for k in range(len(into))},
        compiler_params=pltpu.CompilerParams(vmem_limit_bytes=56 * 2**20),
        cost_estimate=BESIDE,
        name="grad_beside",
    )(left, right, *into)


def tn_kernel(left_ref, right_ref, out_ref):
    out_ref[...] = mm_tn(left_ref[...], right_ref[...]).astype(bf16)


def plain_beside(left, right):
    (depth, rows), columns = left.shape, right.shape[1]
    tile = 2 * BLOCK
    return pl.pallas_call(
        tn_kernel,
        grid=(rows // tile,),
        in_specs=[
            pl.BlockSpec((depth, tile), lambda i: (0, i)),
            pl.BlockSpec(right.shape, lambda i: (0, 0)),
        ],
        out_specs=pl.BlockSpec((tile, columns), lambda i: (i, 0)),
        out_shape=jax.ShapeDtypeStruct((rows, columns), bf16),
        compiler_params=pltpu.CompilerParams(vmem_limit_bytes=56 * 2**20),
        cost_estimate=BESIDE,
        name="plain_beside",
    )(left, right)


def nt_kernel(left_ref, right_ref, out_ref):
    out_ref[...] = mm_nt(left_ref[...], right_ref[...]).astype(bf16)


def product_beside(left, right):
    (rows, depth), columns = left.shape, right.shape[0]
    tile = 2 * BLOCK
    return pl.pallas_call(
        nt_kernel,
        grid=(columns // tile,),
        in_specs=[
            pl.BlockSpec(left.shape, lambda i: (0, 0)),
            pl.BlockSpec((tile, depth), lambda i: (i, 0)),
        ],
        out_specs=pl.BlockSpec((rows, tile), lambda i: (0, i)),
        out_shape=jax.ShapeDtypeStruct((rows, columns), bf16),
        compiler_params=pltpu.CompilerParams(vmem_limit_bytes=56 * 2**20),
        cost_estimate=BESIDE,
        name="product_beside",
    )(left, right)


def mid_kernel(hat_ref, up_ref, gate_ref, dh_ref, hidden_ref, dg_ref, du_ref):
    up = mm(hat_ref[...], up_ref[...])
    gate, d_hidden = gate_ref[...], dh_ref[...]
    sigma = 1.0 / (1.0 + jnp.exp(-gate))
    swish = gate * sigma
    hidden_ref[...] = (swish * up).astype(bf16)
    dg_ref[...] = (d_hidden * up * (sigma + swish * (1.0 - sigma))).astype(bf16)
    du_ref[...] = (d_hidden * swish).astype(bf16)


def mid_layer(hat, up_weight, gate, d_hidden):
    (rows, depth), columns = hat.shape, up_weight.shape[1]
    tile = min(2 * BLOCK, columns)
    spec = pl.BlockSpec((rows, tile), lambda i: (0, i))
    return pl.pallas_call(
        mid_kernel,
        grid=(columns // tile,),
        in_specs=[
            pl.BlockSpec(hat.shape, lambda i: (0, 0)),
            pl.BlockSpec((depth, tile), lambda i: (0, i)),
            spec,
            spec,
        ],
        out_specs=[spec] * 3,
        out_shape=[jax.ShapeDtypeStruct((rows, columns), bf16)] * 3,
        compiler_params=pltpu.CompilerParams(vmem_limit_bytes=56 * 2**20),
        cost_estimate=pl.CostEstimate(
            flops=2 * rows * depth * columns, bytes_accessed=20 * rows * columns, transcendentals=rows * columns
        ),
        name="mid_layer",
    )(hat, up_weight, gate, d_hidden)


def pair_kernel(a_ref, b_ref, c_ref, d_ref, out_ref):
    out_ref[...] = (mm_nt(a_ref[...], b_ref[...]) + mm_nt(c_ref[...], d_ref[...])).astype(bf16)


def pair_product(a, b, c, d):
    (rows, depth), columns = a.shape, b.shape[0]
    tile = 2 * BLOCK
    whole = pl.BlockSpec(a.shape, lambda i: (0, 0))
    part = pl.BlockSpec((tile, depth), lambda i: (i, 0))
    return pl.pallas_call(
        pair_kernel,
        grid=(columns // tile,),
        in_specs=[whole, part, whole, part],
        out_specs=pl.BlockSpec((rows, tile), lambda i: (0, i)),
        out_shape=jax.ShapeDtypeStruct((rows, columns), bf16),
        compiler_params=pltpu.CompilerParams(vmem_limit_bytes=56 * 2**20),
        cost_estimate=pl.CostEstimate(
            flops=4 * rows * depth * columns, bytes_accessed=12 * rows * columns, transcendentals=0
        ),
        name="pair_product",
    )(a, b, c, d)


def after(value, *others):
    return lax.optimization_barrier((value, *others))[0]


def flip(value, mask):
    count = lax.axis_size("dp")
    return lax.ppermute(value, "dp", [(i, i ^ mask) for i in range(count)])


def shift(value, step):
    count = lax.axis_size("tensor")
    return lax.ppermute(value, "tensor", [(i, (i + step) % count) for i in range(count)])


def cross(value, forward):
    masks = (2, 4) if forward else (4, 2)
    return lax.ppermute(value, "dp", [(i, i ^ masks[i % 2]) for i in range(8)])


def gather_order(here, count):
    if count != 8:
        return here ^ jnp.arange(count, dtype=jnp.int32)
    first = jnp.where(here % 2 == 0, 2, 4)
    masks = [0, 1, first, first ^ 1, 6, 7 ^ first, 6 ^ first, 7]
    return here ^ jnp.stack([jnp.asarray(mask, jnp.int32) for mask in masks])


class Order:
    def __init__(self):
        self.last = ()

    def run(self, work, *inputs):
        inputs, _ = lax.optimization_barrier((inputs, self.last))
        result = work(*inputs)
        self.last = jax.tree.leaves(result)
        return result

    def wait(self, *moving):
        moving, _ = lax.optimization_barrier((moving, self.last))
        self.last = jax.tree.leaves(moving)
        return moving if len(moving) > 1 else moving[0]


def double(own):
    bit = 1
    while bit < lax.axis_size("dp"):
        own = jnp.concatenate([own, flip(own, bit)], 0)
        bit *= 2
    return own


class Gather:
    def __init__(self, order, own):
        self.order, self.own, self.count = order, own, lax.axis_size("dp")

    def pair(self):
        if self.count == 8:
            self.beside = flip(self.own, 1)

    def begin(self, own_too=True):
        if self.count == 8:
            if own_too:
                self.own, self.beside = self.order.wait(self.own, self.beside)
                self.first = cross(self.own, True)
            else:
                self.beside = self.order.wait(self.beside)
            self.second = cross(self.beside, True)

    def early(self):
        if self.count == 8:
            self.first = cross(self.own, True)

    def middle(self, with_second=False):
        if self.count == 8:
            if with_second:
                self.first, self.second = self.order.wait(self.first, self.second)
            else:
                self.first = self.order.wait(self.first)
            self.third = cross(self.first, False)

    def late(self):
        if self.count == 8:
            self.second, self.third = self.order.wait(self.second, self.third)
            self.flipped = [flip(piece, 1) for piece in (self.first, self.second, self.third)]

    def end(self, groups=1):
        if self.count == 8:
            flipped = self.order.wait(*self.flipped)
            pieces = (self.own, self.beside, self.first, self.second, self.third, *flipped)
            whole = self.order.run(lambda *pieces: stack(pieces, groups), *pieces)
            return whole if groups > 1 else whole[0]
        return double(self.own)


class Ring:
    def __init__(self, order, terms, owner_part):
        self.order, self.count = order, lax.axis_size("tensor")
        self.terms, self.part, self.stage = terms, owner_part, 1
        sent = order.run(lambda terms: self.part(terms, 1), terms)
        self.moving = shift(sent, 1)

    def step(self):
        if self.stage == self.count:
            return
        self.stage += 1
        arrived = self.arrived = self.order.wait(self.moving)

        def add(arrived, terms):
            total = arrived.astype(f32) + self.part(terms, self.stage % self.count).astype(f32)
            return total.astype(bf16) if self.stage < self.count else total

        total = self.order.run(add, arrived, self.terms)
        if self.stage < self.count:
            self.moving = shift(total, 1)
        else:
            self.result = total

    def finish(self):
        while self.stage < self.count:
            self.step()
        return self.result


class Line:
    def __init__(self, order, terms, owner_part):
        self.order, self.terms, self.part = order, terms, owner_part
        self.count, self.place, self.stage = lax.axis_size("tensor"), lax.axis_index("tensor"), 0
        self.step()

    def send(self, value, up):
        pairs = [(i, i + 1) for i in range(self.count - 1) if i < self.stage]
        if not up:
            pairs = [(self.count - 1 - i, self.count - 1 - j) for i, j in pairs]
        return lax.ppermute(value, "tensor", pairs)

    def step(self):
        if self.stage == self.count:
            return
        arrived = self.order.wait(*self.moving) if self.stage else ()
        self.stage += 1
        if self.stage == self.count:
            self.result = self.order.run(
                lambda terms, up, down: self.part(terms, 0).astype(f32)
                + up.astype(f32)
                + down.astype(f32),
                self.terms,
                *arrived,
            )
            return
        ahead = self.count - self.stage
        owners = jnp.minimum(self.place + ahead, self.count - 1), jnp.maximum(self.place - ahead, 0)

        def add(terms, *arrived):
            values = [self.part(terms, (self.place - owner) % self.count) for owner in owners]
            if arrived:
                values = [a.astype(f32) + b.astype(f32) for a, b in zip(values, arrived)]
            return [value.astype(bf16) for value in values]

        up, down = self.order.run(add, self.terms, *arrived)
        self.moving = self.send(up, True), self.send(down, False)

    def finish(self):
        while self.stage < self.count:
            self.step()
        return self.result


class Spread:
    def __init__(self, order, own):
        self.order, self.own = order, own
        self.count, self.place, self.stage = lax.axis_size("tensor"), lax.axis_index("tensor"), 0
        self.arrived = [(own, own)]
        self.go()

    def go(self):
        up, down = self.arrived[-1]
        pairs = [(i, i + 1) for i in range(self.count - 1) if i >= self.stage]
        back = [(self.count - 1 - i, self.count - 1 - j) for i, j in pairs]
        self.moving = lax.ppermute(up, "tensor", pairs), lax.ppermute(down, "tensor", back)
        self.stage += 1

    def step(self):
        if len(self.arrived) < self.count:
            self.arrived.append(self.order.wait(*self.moving))
            if self.stage < self.count - 1:
                self.go()

    def whole(self, dtype):
        rows, width = self.own.shape
        result = jnp.zeros((rows * self.count, width), dtype)
        for t in range(self.count):
            value = self.own
            if t:
                up, down = self.arrived[t][0], self.arrived[self.count - t][1]
                value = jnp.where(self.place >= t, up, down)
            start = (self.place - t) % self.count * rows
            result = lax.dynamic_update_slice(result, value.astype(dtype), (start, 0))
        return result


def local(
    layer_input,
    output_cotangent,
    block_ids,
    attention_gain,
    query_weight,
    key_weight,
    value_weight,
    output_weight,
    feedforward_gain,
    gate_weight,
    up_weight,
    down_weight,
):
    tokens, width = layer_input.shape
    here = lax.axis_index("dp")
    place = lax.axis_index("tensor")
    dp_count = lax.axis_size("dp")
    ring = lax.axis_size("tensor")
    part = tokens // ring
    columns = query_weight.shape[1]
    heads_here = columns // HEAD_DIM
    heads = heads_here * ring

    near_order = gather_order(here, dp_count)
    true_order = jnp.argsort(near_order).astype(jnp.int32)

    def token_part(values, owner):
        return lax.dynamic_slice_in_dim(values, owner * part, part, 0)

    gain_one = attention_gain.astype(f32)[:, None]
    gain_two = feedforward_gain.astype(f32)[:, None]
    qkv_weight = jnp.concatenate([query_weight, key_weight, value_weight], 1).astype(f32)
    order = Order()
    run, wait = order.run, order.wait

    def ring_part(values, t):
        return token_part(values, (place - t) % ring)

    qkv_gather = Gather(order, run(lambda w, g: (w * g).astype(bf16), qkv_weight, gain_one))
    qkv_gather.early()
    qkv_gather.pair()
    out_moving = [shift(output_weight, step) for step in range(1, ring)]
    gate_own = run(lambda w, g: (w.astype(f32) * g).astype(bf16), gate_weight, gain_two)
    up_own = run(lambda w, g: (w.astype(f32) * g).astype(bf16), up_weight, gain_two)
    qkv_gather.begin(False)
    hat, inputs, hat_true = run(normed_in_order, layer_input, near_order)
    qkv_gather.middle(True)
    out_pieces = wait(*out_moving)
    both_own = run(
        lambda down, *pieces: (jnp.transpose(jnp.concatenate(pieces, 0)), jnp.transpose(down)),
        down_weight,
        output_weight,
        *out_pieces,
    )
    paired = dp_count == 8 and both_own[0].shape == both_own[1].shape
    both_gather = Gather(order, jnp.concatenate(both_own, 0) if paired else both_own[0])
    both_gather.pair()
    gate_gather, up_gather = Gather(order, gate_own), Gather(order, up_own)
    qkv_gather.late()
    both_gather.begin()
    qkv_all = qkv_gather.end()

    qkv = run(mm, hat, qkv_all)
    cosine, sine = rope_tables(tokens)
    ends = last_visible(block_ids[0])
    queries, keys, values, attended, stats = run(attend_forward, qkv, ends, cosine, sine)
    moving = shift(attended, 1)
    pieces = [attended]
    gate_gather.pair()
    up_gather.pair()
    cot = run(in_order, output_cotangent, near_order)
    both_gather.middle(True)
    while len(pieces) < ring - 1:
        pieces.append(wait(moving))
        moving = shift(pieces[-1], 1)
        if len(pieces) == 2:
            gate_gather.begin()
            gate_gather.middle(True)
    up_gather.begin()
    both_gather.late()
    if paired:
        out_all, down_all = both_gather.end(2)
    else:
        out_all, down_all = both_gather.end(), double(both_own[1])
    most = jnp.concatenate(pieces, 1)
    resid_most = run(
        lambda inputs, most, weight: inputs.astype(f32) + mm_nt(most, weight[:, : most.shape[1]]),
        inputs,
        most,
        out_all,
    )
    pieces.append(wait(moving))
    gate_gather.late()

    resid_part, hat_two, hat_two_true = run(
        lambda most, last, weight, place: resid_and_norm(
            most, last, weight[:, weight.shape[1] - columns :], place, true_order, part
        ),
        resid_most,
        pieces[-1],
        out_all,
        place,
    )
    up_gather.middle()
    d_hidden = run(mm, cot, down_all)
    gate_all = gate_gather.end()
    up_gather.late()
    gate = run(mm, hat_two, gate_all)
    up_all = up_gather.end()

    hidden, d_gate, d_up = run(mid_layer, hat_two, up_all, gate, d_hidden)
    d_mid = run(pair_product, d_gate, gate_all, d_up, up_all)

    def scaled(total, weight, gain):
        total = total.astype(f32)
        return total * gain, jnp.sum(total * weight.astype(f32), 1)

    def to_sum(grad, *before):
        grad = after(grad, *before) if before else grad
        return lax.psum_scatter(grad, "dp", scatter_dimension=0, tiled=True)

    back = Ring(order, d_mid, ring_part)
    local_peak = jnp.max(stats[:, 2:4], -1).reshape(heads_here)
    peaks = [local_peak, 1]

    def peak_step():
        if peaks[1] < dp_count:
            peaks[0] = jnp.maximum(peaks[0], wait(flip(peaks[0], peaks[1])))
            peaks[1] *= 2

    gate_grad = run(plain_beside, hat_two_true, d_gate)
    peak_step()
    back.step()
    gate_moving = to_sum(gate_grad, back.arrived)
    up_grad = run(plain_beside, hat_two_true, d_up)
    peak_step()
    back.step()
    up_moving = to_sum(up_grad, gate_grad, back.arrived)
    mlp = run(product_beside, hidden, down_all)
    down_grad = run(plain_beside, output_cotangent, hidden)
    peak_step()
    scaled_two = back.finish()
    down_moving = to_sum(down_grad, up_grad, back.arrived)
    while peaks[1] < dp_count:
        peak_step()
    local_peak = peaks[0]
    forth = Ring(order, mlp, ring_part)

    def first_norm_back(scaled, resid, cot):
        inverse = lax.rsqrt(jnp.mean(resid * resid, -1, keepdims=True) + norm_epsilon)
        back = resid * inverse**3 * jnp.mean(scaled * resid, -1, keepdims=True)
        return token_part(cot, place).astype(f32) + inverse * scaled - back

    d_resid = run(first_norm_back, scaled_two, resid_part, cot)
    d_attn = d_resid.astype(bf16)
    d_att = run(lambda a, b: mm(a, b).astype(bf16), d_attn, out_all)
    d_moving = [shift(d_att[:, t * columns : (t + 1) * columns], -t) for t in range(1, ring)]
    def unite(*pieces):
        whole = jnp.zeros((tokens, columns), bf16)
        for t, piece in enumerate(pieces):
            whole = lax.dynamic_update_slice(whole, piece, ((place + t) % ring * part, 0))
        return whole

    d_pieces = wait(*d_moving)
    d_attended = run(unite, d_att[:, :columns], *d_pieces)

    def in_true_order(*pieces):
        parts = [token_part(piece, place) for piece in pieces[::-1]]
        both = jnp.concatenate(parts + parts, 0)
        whole = lax.dynamic_slice_in_dim(both, (ring - 1 - place) * part, tokens, 0)
        return jnp.concatenate(jnp.split(whole, ring, 0), 1)

    forth.step()

    def in_true_order(*pieces):
        parts = [token_part(piece, place) for piece in pieces[::-1]]
        both = jnp.concatenate(parts + parts, 0)
        whole = lax.dynamic_slice_in_dim(both, (ring - 1 - place) * part, tokens, 0)
        return jnp.concatenate(jnp.split(whole, ring, 0), 1)

    parts = run(
        attend_backward, queries, keys, values, attended, d_attended, stats, ends, cosine, sine
    )
    forth.step()
    d_qkv, d_in = run(
        lambda weight, *parts: (
            jnp.concatenate(parts, 1),
            mm_nt(jnp.concatenate(parts, 1), weight).astype(bf16),
        ),
        qkv_all,
        *parts,
    )
    qkv_grad = run(plain_beside, hat_true, d_qkv)
    out_part = run(
        lambda a, b, c: in_order((a + b).astype(bf16), c), resid_part, forth.finish(), true_order
    )
    qkv_moving = to_sum(qkv_grad, down_grad, forth.arrived)
    layer_out = Spread(order, out_part)
    att_part = run(in_true_order, *pieces)
    d_attn_true = run(in_order, d_attn, true_order)
    out_grad = run(plain_beside, d_attn_true, att_part)
    layer_out.step()
    back = Line(order, d_in, ring_part)
    out_moving = to_sum(out_grad, qkv_grad, *layer_out.arrived[1])
    back.step()
    layer_out.step()
    back.step()
    while len(layer_out.arrived) < ring:
        layer_out.step()
    scaled_one = back.finish()

    def second_norm_back(scaled, inputs, d_resid, true_order):
        values = token_part(inputs, place).astype(f32)
        inverse = lax.rsqrt(jnp.mean(values * values, -1, keepdims=True) + norm_epsilon)
        back = values * inverse**3 * jnp.mean(scaled * values, -1, keepdims=True)
        return in_order((d_resid + inverse * scaled - back).astype(bf16), true_order)

    in_part = run(second_norm_back, scaled_one, inputs, d_resid, true_order)
    moving, in_pieces = shift(in_part, 1), [in_part]
    layer_output = run(lambda: layer_out.whole(bf16))
    input_grad = jnp.zeros((tokens, width), f32)

    def place_piece(whole, piece):
        start = (place - len(in_pieces) + 1) % ring * part
        return lax.dynamic_update_slice(whole, piece.astype(f32), (start, 0))

    input_grad = run(place_piece, input_grad, in_part)
    while len(in_pieces) < ring:
        in_pieces.append(wait(moving))
        if len(in_pieces) < ring:
            moving = shift(in_pieces[-1], 1)
            input_grad = run(place_piece, input_grad, in_pieces[-1])
            if len(in_pieces) == 2:
                gate_result = run(scaled, wait(gate_moving), gate_weight, gain_two)
                up_result = run(scaled, wait(up_moving), up_weight, gain_two)
                down_result = run(lambda a: jnp.transpose(a.astype(f32)), wait(down_moving))
            else:
                qkv_result = run(scaled, wait(qkv_moving), qkv_weight, gain_one)
                out_rows = run(jnp.transpose, wait(out_moving))

    small = jnp.concatenate(
        [
            qkv_result[1],
            gate_result[1] + up_result[1],
            local_peak,
            jnp.zeros((LANES - heads_here,), f32),
        ]
    )
    small_moving = [shift(small, step) for step in range(1, ring)]

    def heads_of(owner):
        return lax.dynamic_slice_in_dim(out_rows, owner * columns, columns, 0)

    out_moving = [shift(heads_of((place + step) % ring), step) for step in range(1, ring)]
    input_grad = run(place_piece, input_grad, in_pieces[-1])
    smalls = [small, *wait(*small_moving)]
    share = width // dp_count
    peak_pieces = [piece[2 * share : 2 * share + heads_here] for piece in smalls]
    gain_sum = jnp.take(jnp.stack(smalls), (place - jnp.arange(ring)) % ring, axis=0)
    gain_sum = jnp.sum(gain_sum[:, : 2 * share].reshape(ring, 2, share), 0)
    output_grad = heads_of(place).astype(f32)
    for moved in wait(*out_moving):
        output_grad = output_grad + moved.astype(f32)
    qkv_grad = qkv_result[0]

    spots = (place - jnp.arange(heads) // heads_here) % ring * heads_here
    head_maxima = jnp.concatenate(peak_pieces)[spots + jnp.arange(heads) % heads_here]
    factor = jnp.sqrt(clip_tau / jnp.maximum(local_peak, clip_tau))
    factors = jnp.repeat(factor, HEAD_DIM)[None, :]
    query_clipped = (query_weight.astype(f32) * factors).astype(bf16)
    key_clipped = (key_weight.astype(f32) * factors).astype(bf16)

    return (
        layer_output,
        input_grad,
        gain_sum[0],
        qkv_grad[:, :columns],
        qkv_grad[:, columns : 2 * columns],
        qkv_grad[:, 2 * columns :],
        output_grad,
        gain_sum[1],
        gate_result[0],
        up_result[0],
        down_result,
        head_maxima,
        query_clipped,
        key_clipped,
    )


def solution(mesh):
    in_specs = (
        P("dp", None),
        P("dp", None),
        P("dp", None),
        P("dp"),
        P("dp", "tensor"),
        P("dp", "tensor"),
        P("dp", "tensor"),
        P("tensor", "dp"),
        P("dp"),
        P("dp", "tensor"),
        P("dp", "tensor"),
        P("tensor", "dp"),
    )
    out_specs = (
        P("dp", None),
        P("dp", None),
        P("dp"),
        P("dp", "tensor"),
        P("dp", "tensor"),
        P("dp", "tensor"),
        P("tensor", "dp"),
        P("dp"),
        P("dp", "tensor"),
        P("dp", "tensor"),
        P("tensor", "dp"),
        P(),
        P("dp", "tensor"),
        P("dp", "tensor"),
    )
    return jax.shard_map(local, mesh=mesh, in_specs=in_specs, out_specs=out_specs, check_vma=False)
```
